256 devices in a mesh: slab: 2 (over core), grp: 16 (over y, x), col: 8 (over z).
Axes of the slice: x: 4, y: 4, z: 8, core: 2. Of those that a mesh axis runs over, the one named last changes fastest.
Arguments:
- fine_blocks: bfloat16 [2048, 27, 64, 64], P(('slab', 'grp', 'col')), may hold values from -4 to 4
- prolong: bfloat16 [2048, 64, 64], P(('slab', 'grp', 'col')), may hold values from -2 to 2
- column_ids: int32 [2048, 27], P(('slab', 'grp', 'col')), may hold values from 0 to 159
- aggregate_ids: int32 [2048], P(('slab', 'grp', 'col')), may hold values from 0 to 15, as said below
- live_rows: int32 [256], P(('slab', 'grp', 'col')), may hold values from 1 to 8, 1536 in all
Outputs:
- coarse: float32 [256, 80, 64, 64], P(('slab', 'grp', 'col'))
The draws below stay inside these ranges and needn't reach their ends.
Inputs may be any that keep to these rules, and one draw needn't show every extreme that they name: `aggregate_ids`: among the 8 rows of one device no aggregate is named by more than 2 rows, and one aggregate is named by exactly 2 rows.
All inputs are finite; a program needn't handle non-finite values. No bound on the sum of `live_rows` on one device may be relied on, other than what follows from the above.
Results may differ from the reference program's by a relative error of at most 0.00035.
Values may be sent and summed in bfloat16 or wider, within the bound.
A program may use at most 256 MiB of HBM per device.

```python
import math
import jax
import jax.numpy as jnp
import numpy as np
from jax import lax

B = 64
RB = 8
KA = 27
NFINE = 2048
MOST = 2
N_SLAB = 2
N_GRP = 16
N_COL = 8
DEVICES = 256


def device_aggregates(key):
    first_key, rest_key, order_key = jax.random.split(key, 3)
    chosen = jax.random.randint(first_key, (), 0, N_GRP).astype(jnp.int32)
    others = (jnp.arange(N_GRP - 1, dtype=jnp.int32) + chosen + 1) % N_GRP
    pool = jnp.repeat(others, MOST)
    pool = jax.random.permutation(rest_key, pool)[:RB - MOST]
    picked = jnp.concatenate([jnp.full((MOST,), 0, jnp.int32) + chosen, pool.astype(jnp.int32)], 0)
    return jax.random.permutation(order_key, picked).astype(jnp.int32)


def draw_aggregate_ids(key, part):
    key = jax.random.fold_in(key, 7)
    device_keys = jax.random.split(key, DEVICES)
    return jax.vmap(device_aggregates)(device_keys).reshape(-1).astype(jnp.int32)


def set_ends(entries, key, smallest, largest):
    extent = entries.shape
    place = [jax.random.randint(jax.random.fold_in(key, axis), (), 0, extent[axis]) for axis in range(len(extent))]
    entries = entries.at[tuple(place)].set(smallest)
    longest = extent.index(max(extent))
    place[longest] = (place[longest] + 1) % extent[longest]
    return entries.at[tuple(place)].set(largest)


def level_of(key, shape, pieces, least, high):
    gain, own = 1.0, jax.random.fold_in(key, 6)
    for axis_at, shards_of in pieces:
        steps = jnp.exp(jax.random.uniform(jax.random.fold_in(own, axis_at), (shards_of,), jnp.float32, least / len(pieces), high / len(pieces)))
        gain = gain * jnp.repeat(steps, shape[axis_at] // shards_of).reshape([-1 if axis == axis_at else 1 for axis in range(len(shape))])
    return gain


def profile(count, total, limit, skew):
    weights = [(1 << 20) // math.isqrt(standing ** skew) + 1 for standing in range(2, count + 1)]
    rest, holding = total - limit - (count - 1), [1] * (count - 1)
    while rest > 0:
        candidates = [i for i in range(count - 1) if holding[i] < limit]
        whole, remaining = sum([weights[i] for i in candidates]), rest
        for i in candidates:
            more = min(limit - holding[i], max(1, remaining * weights[i] // whole), rest)
            holding[i] = holding[i] + more
            rest = rest - more
    return np.array([limit] + holding)


def ragged_sizes(own_key, number_of, total, most, lean):
    if number_of == 2:
        one = jax.random.randint(own_key, (), max(1, total - most), min(most, total - 1) + 1)
        return jnp.stack([one, total - one])
    lengths = jnp.asarray(profile(number_of, total, most, lean), jnp.int32)
    pairs = (number_of - 1) // 2
    donor, receiver = lengths[1:1 + 2 * pairs:2], lengths[2:2 + 2 * pairs:2]
    slack = jnp.minimum(donor - 1, most - receiver)
    moved = jax.random.randint(jax.random.fold_in(own_key, 1), (pairs,), 0, 1 << 20) % (slack + 1)
    lengths = lengths.at[1:1 + 2 * pairs:2].set(donor - moved).at[2:2 + 2 * pairs:2].set(receiver + moved)
    return lengths[jax.random.permutation(jax.random.fold_in(own_key, 2), number_of)]


def noise(own_key, extent, scale, reach, shards=(), kind=jnp.bfloat16):
    gain = level_of(own_key, extent, shards, -0.22, 0.18) if shards else 1.0
    entries = jax.random.normal(own_key, extent, jnp.float32) * scale * gain
    return jnp.minimum(jnp.maximum(entries, -reach), reach).astype(kind)


def setup_inputs(seed: int = 0) -> dict:
    key_list = jax.random.split(jax.random.key(seed), 6)
    fine_blocks = noise(key_list[0], (NFINE, KA, B, B), 0.25, 4.0, ((0, 256),))
    prolong = noise(key_list[1], (NFINE, B, B), 0.125, 2.0, ((0, 256),))
    column_ids = set_ends(jax.random.randint(key_list[2], (NFINE, KA), 0, (N_GRP + 4) * RB), jax.random.fold_in(key_list[2], 1), 0, ((N_GRP + 4) * RB) - 1).astype(jnp.int32)
    aggregate_ids = draw_aggregate_ids(jax.random.fold_in(key_list[5], 71), 0)
    live_rows = ragged_sizes(key_list[4], DEVICES, DEVICES * RB * 3 // 4, RB, 2).astype(jnp.int32)
    return {"fine_blocks": fine_blocks, "prolong": prolong, "column_ids": column_ids, "aggregate_ids": aggregate_ids, "live_rows": live_rows}


def reference(fine_blocks, prolong, column_ids, aggregate_ids, live_rows):
    groups = N_GRP
    width = 5 * groups
    rows = jnp.arange(DEVICES * RB, dtype=jnp.int32)
    device = rows // RB
    local = rows % RB
    live_mask = (local < live_rows[device]).astype(jnp.bfloat16)
    masked = prolong * live_mask[:, None, None]
    slab_idx = device // (N_GRP * N_COL)
    grp_idx = (device // N_COL) % N_GRP
    col_idx = device % N_COL
    split = N_GRP * RB
    inside = column_ids < split
    extra = jnp.maximum(column_ids - split, 0)
    direction = extra // RB
    slab_step = jnp.where(direction == 0, -1, jnp.where(direction == 1, 1, 0)).astype(jnp.int32)
    col_step = jnp.where(direction == 2, -1, jnp.where(direction == 3, 1, 0)).astype(jnp.int32)
    tslab = jnp.where(inside, slab_idx[:, None], slab_idx[:, None] + slab_step)
    tcol = jnp.where(inside, col_idx[:, None], col_idx[:, None] + col_step)
    tgrp = jnp.where(inside, column_ids // RB, grp_idx[:, None])
    trow = jnp.where(inside, column_ids % RB, extra % RB)
    valid = (tslab >= 0) & (tslab < N_SLAB) & (tcol >= 0) & (tcol < N_COL)
    target = ((jnp.clip(tslab, 0, N_SLAB - 1) * N_GRP + tgrp) * N_COL + jnp.clip(tcol, 0, N_COL - 1)) * RB + trow
    target = target.astype(jnp.int32)
    slot = jnp.where(inside, 0, direction + 1) * groups + jnp.where(valid, aggregate_ids[target], 0)
    owner = (slab_idx * N_GRP + aggregate_ids) * N_COL + col_idx
    keys = (owner[:, None] * width + slot).astype(jnp.int32)

    def step(total, dev):
        start = (dev * RB).astype(jnp.int32)
        blocks = lax.dynamic_slice_in_dim(fine_blocks, start, RB, 0)
        tgt = lax.dynamic_slice_in_dim(target, start, RB, 0)
        ok = lax.dynamic_slice_in_dim(valid, start, RB, 0)
        own = lax.dynamic_slice_in_dim(masked, start, RB, 0).astype(jnp.float32)
        key = lax.dynamic_slice_in_dim(keys, start, RB, 0)
        picked = jnp.where(ok[:, :, None, None], masked[tgt], jnp.zeros((), jnp.bfloat16))
        products = jnp.einsum("rkab,rkbc->rkac", blocks.astype(jnp.float32), picked.astype(jnp.float32))
        triple = jnp.einsum("rba,rkbc->rkac", own, products, precision=lax.Precision.HIGHEST)
        total = total.at[key.reshape(-1)].add(triple.reshape(-1, B, B))
        return total, None

    start_total = jnp.zeros((DEVICES * width, B, B), jnp.float32)
    total, unused = lax.scan(step, start_total, jnp.arange(DEVICES, dtype=jnp.int32))
    return total.reshape(DEVICES, width, B, B)
```

```python
import functools

import jax
import jax.numpy as jnp
from jax import lax
from jax.experimental import pallas as pl
from jax.experimental.pallas import tpu as pltpu
from jax.sharding import PartitionSpec as P

MESH = pl.DeviceIdType.MESH
GRP, SIDE, NCOL = 16, 4, 8
RB, KA, B = 8, 27, 64
KP = 28
CHUNKS, PER = 2, 4
CR = KP * PER
WIDTH = 80
TILES = 160
MSG = 272
HALF = (pl.ds(0, 144), pl.ds(144, 128))
FULL = 32760.0
F32, BF16 = jnp.float32, jnp.bfloat16


def code(x, inverse):
    v = jnp.sqrt(jnp.abs(x) * inverse) + 0.5
    return jnp.where(x < 0, -v, v).astype(jnp.int32).astype(jnp.int16)


def remote(src, dst, send, recv, where):
    return pltpu.make_async_remote_copy(
        src_ref=src, dst_ref=dst, send_sem=send, recv_sem=recv, device_id=where, device_id_type=MESH
    )


def kernel(
    blocks_hbm, prolong, ids_vec, ids, aggs, live,
    result,
    blocks, tiles, table, flipped, u, ids_row, stage, out1, got1, side_out, side, total, out2, scale_out, got2, scale2,
    block_sem, ag_send, ag_recv, near_send, near_recv,
    d_send, d_recv, s_send, s_recv, e_send, e_recv, f_send, f_recv,
):
    s, g, c = lax.axis_index("slab"), lax.axis_index("grp"), lax.axis_index("col")
    gy, gx = g // SIDE, lax.rem(g, SIDE)
    bar = pltpu.get_barrier_semaphore()
    for p in range(1, GRP):
        pl.semaphore_signal(bar, inc=1, device_id={"grp": lax.rem(g + p, GRP)}, device_id_type=MESH)
    pl.semaphore_signal(bar, inc=1, device_id={"slab": 1 - s}, device_id_type=MESH)

    @pl.when(c > 0)
    def _():
        pl.semaphore_signal(bar, inc=1, device_id={"col": c - 1}, device_id_type=MESH)

    @pl.when(c < NCOL - 1)
    def _():
        pl.semaphore_signal(bar, inc=1, device_id={"col": c + 1}, device_id_type=MESH)

    block_copy = pltpu.make_async_copy(blocks_hbm, blocks, block_sem)
    block_copy.start()

    alive = jnp.full((B, B), live[0], jnp.int32)
    for r in range(0, RB, 2):
        left, right = (
            jnp.where(alive > r + d, prolong[r + d].astype(F32), 0.0) for d in range(2)
        )
        tiles[g, 32 * r : 32 * r + B, :] = jnp.concatenate([left, right], axis=1).astype(BF16)
        flipped[r] = left.T.astype(BF16)
        flipped[r + 1] = right.T.astype(BF16)
    sub16 = lax.broadcasted_iota(jnp.int32, (16, 128), 0)
    agg_rows = jnp.zeros((16, 128), F32)
    for r in range(RB):
        agg_rows = jnp.where(sub16 == r, aggs[r].astype(F32), agg_rows)
    tiles[g, 256:MSG, :] = agg_rows.astype(BF16)

    tiles[GRP + s] = jnp.zeros((MSG, 128), BF16)

    @pl.when(c == 0)
    def _():
        tiles[GRP + 2] = jnp.zeros((MSG, 128), BF16)

    @pl.when(c == NCOL - 1)
    def _():
        tiles[GRP + 3] = jnp.zeros((MSG, 128), BF16)

    cols = (c + NCOL - 1) // NCOL + (2 * NCOL - 2 - c) // NCOL
    pl.semaphore_wait(bar, GRP + cols)

    sends = []

    def spread(slot, half, y, x, source):
        copy = remote(
            tiles.at[slot, HALF[half]],
            tiles.at[slot, HALF[half]],
            ag_send.at[len(sends)],
            ag_recv.at[source * 2 + half],
            {"grp": y * SIDE + x},
        )
        copy.start()
        sends.append(copy)

    def arrived(dy, dx, half):
        slot = lax.rem(gy + dy, SIDE) * SIDE + lax.rem(gx + dx, SIDE)
        remote(
            tiles.at[slot, HALF[half]], tiles.at[slot, HALF[half]],
            ag_send.at[0], ag_recv.at[(dy * SIDE + dx) * 2 + half], {"grp": lax.rem(g + 1, GRP)},
        ).wait_recv()
        return slot

    for d in (1, 3, 2):
        back = SIDE - d
        spread(g, 0, gy, lax.rem(gx + d, SIDE), back)
        spread(g, 1, lax.rem(gy + d, SIDE), gx, back * SIDE)
    for d in (1, 3, 2):
        back = SIDE - d
        spread(g, 1, gy, lax.rem(gx + d, SIDE), back)
        spread(g, 0, lax.rem(gy + d, SIDE), gx, back * SIDE)

    def near(k, slot, where):
        return remote(tiles.at[g], tiles.at[slot], near_send.at[k], near_recv.at[k], where)

    near(0, GRP + s, {"slab": 1 - s}).start()

    @pl.when(c < NCOL - 1)
    def _():
        near(1, GRP + 2, {"col": c + 1}).start()

    @pl.when(c > 0)
    def _():
        near(2, GRP + 3, {"col": c - 1}).start()

    block_copy.wait()

    def u_row(i, carry):
        for k in range(0, KP, 2):
            left = jnp.dot(flipped[i], blocks[i, k], preferred_element_type=F32)
            if k + 1 < KA:
                right = jnp.dot(flipped[i], blocks[i, k + 1], preferred_element_type=F32)
            else:
                right = jnp.zeros((B, B), F32)
            value = jnp.concatenate([left, right], axis=1)
            high = value.astype(BF16)
            u[i, k // 2, 0:B, :] = high
            u[i, k // 2, B : 2 * B, :] = (value - high.astype(F32)).astype(BF16)
        return carry

    wide = lax.broadcasted_iota(jnp.int32, (B, 128), 1) < B

    def unfold(slot):
        def pair(n, carry):
            both = tiles[slot, pl.ds(pl.multiple_of(n * B, B), B), :].astype(F32)
            turned = pltpu.roll(both, B, 1)
            at = slot * RB + 2 * n
            table[at] = jnp.where(wide, both, 0.0).astype(BF16)
            table[at + 1] = jnp.where(wide, turned, 0.0).astype(BF16)
            table[TILES + at] = jnp.where(wide, 0.0, turned).astype(BF16)
            table[TILES + at + 1] = jnp.where(wide, 0.0, both).astype(BF16)
            return carry

        lax.fori_loop(0, RB // 2, pair, 0)

    lax.fori_loop(0, 2, u_row, 0)

    for e in (1, 3, 2):
        slot = arrived(0, e, 0)
        for d in (1, 3, 2):
            spread(slot, 0, lax.rem(gy + d, SIDE), gx, (SIDE - d) * SIDE + e)
        slot = arrived(e, 0, 1)
        for d in (1, 3, 2):
            spread(slot, 1, gy, lax.rem(gx + d, SIDE), e * SIDE + SIDE - d)

    lax.fori_loop(2, RB, u_row, 0)
    unfold(g)
    for e in (1, 3, 2):
        unfold(arrived(0, e, 1))
        unfold(arrived(e, 0, 0))
    near(0, GRP + 1 - s, {"slab": 1 - s}).wait_recv()

    @pl.when(c > 0)
    def _():
        near(1, GRP + 2, {"col": c - 1}).wait_recv()

    @pl.when(c < NCOL - 1)
    def _():
        near(2, GRP + 3, {"col": c + 1}).wait_recv()

    for slot in range(GRP, GRP + 4):
        unfold(slot)
    for e in (1, 3, 2):
        for f in (1, 3, 2):
            arrived(e, f, 0)
            unfold(arrived(e, f, 1))

    ids_row[...] = jnp.full((8, 128), -1, jnp.int32)
    ids_row[:, 0:KA] = ids_vec[...]
    lane = lax.broadcasted_iota(jnp.int32, (8, 128), 1)
    sub = lax.broadcasted_iota(jnp.int32, (8, 128), 0)
    for ch in range(CHUNKS):
        q = jnp.full((8, 128), -1, jnp.int32)
        owner = jnp.zeros((8, 128), F32)
        for ii in range(PER):
            i = PER * ch + ii
            row = jnp.broadcast_to(ids_row[i : i + 1, :], (8, 128))
            inside = (lane >= KP * ii) & (lane < KP * (ii + 1))
            q = jnp.where(inside, pltpu.roll(row, KP * ii, 1) if ii else row, q)
            owner = jnp.where(inside, aggs[i].astype(F32), owner)
        slot = jnp.zeros((8, 128), F32)
        for d in range(GRP + 4):
            base = 0 if d < GRP else (d - GRP + 1) * GRP
            named = tiles[d, 256:MSG, :].astype(F32)[0:8]
            slot = slot + jnp.where(q == sub + 8 * d, named + base, 0.0)
        slot = jnp.broadcast_to(jnp.sum(slot, axis=0, keepdims=True), (8, 128))
        key = jnp.where(q < 0, -1.0, owner * WIDTH + slot)
        side_out[ch] = jnp.where(sub == 0, key, 0.0)

    low = lax.broadcasted_iota(jnp.int32, (8, 128), 1) < B

    def piece(ch, p):
        where = lax.bitwise_xor(g, p)
        return (
            remote(out1.at[ch, where], got1.at[ch, g], d_send.at[ch, p], d_recv.at[ch, p], {"grp": where}),
            remote(side_out.at[ch], side.at[ch, g], s_send.at[ch, p], s_recv.at[ch, p], {"grp": where}),
        )

    for ch in range(CHUNKS):
        def t_row(ii, scales, ch=ch):
            i = PER * ch + ii
            top = jnp.zeros((8, 128), F32)
            for k in range(0, KP, 2):
                weights = jnp.concatenate(
                    [table[ids[i, k]], table[TILES + ids[i, min(k + 1, KA - 1)]]], axis=0
                )
                both = jnp.dot(u[i, k // 2], weights, preferred_element_type=F32)
                value = both[0:B] + both[B : 2 * B]
                top = jnp.maximum(top, jnp.max(jnp.abs(value).reshape(8, 8, 128), axis=0))
                for half in range(2):
                    for w in range(2):
                        first = value[32 * w + 8 * half : 32 * w + 8 * half + 8]
                        second = value[32 * w + 16 + 8 * half : 32 * w + 24 + 8 * half]
                        at = CR * (GRP * w + 8 * half) + KP * ii + k
                        stage[pl.ds(at, 8, stride=CR), :] = jnp.where(low, first, pltpu.roll(second, B, 1))
                        stage[pl.ds(at + 1, 8, stride=CR), :] = jnp.where(low, pltpu.roll(first, B, 1), second)
            most = jnp.max(jnp.max(top, axis=1, keepdims=True), axis=0, keepdims=True)
            most = jnp.broadcast_to(most, (8, 128))
            unit = (jnp.maximum(most, 1e-25) * (1.004 / (FULL * FULL))).astype(BF16).astype(F32)
            return tuple(jnp.where(ii == n, unit, scales[n]) for n in range(PER))

        scales = lax.fori_loop(0, PER, t_row, tuple(jnp.zeros((8, 128), F32) for _ in range(PER)))
        unit_row = jnp.zeros((8, 128), F32)
        row_of = lax.broadcasted_iota(jnp.int32, (CR, 128), 0)
        inverse = jnp.zeros((CR, 128), F32)
        for ii in range(PER):
            unit_row = jnp.where((lane >= KP * ii) & (lane < KP * (ii + 1)), scales[ii], unit_row)
            inverse = jnp.where(row_of >= KP * ii, (1.0 / scales[ii])[0:1], inverse)
        side_out[ch] = jnp.where(sub == 1, unit_row, side_out[ch])
        side[ch, g] = side_out[ch]

        def coded(where, ch=ch, inverse=inverse):
            first = code(stage[pl.ds(pl.multiple_of(where * CR, 16), CR), :], inverse)
            second = code(stage[pl.ds(pl.multiple_of((GRP + where) * CR, 16), CR), :], inverse)
            return jnp.concatenate([first, second], axis=1)

        got1[ch, g] = coded(g)

        def emit(p, carry, ch=ch):
            where = lax.bitwise_xor(g, p)
            out1[ch, where] = coded(where)
            data, extra = piece(ch, p)
            extra.start()
            data.start()
            return carry

        lax.fori_loop(1, GRP, emit, 0)

    total[...] = jnp.zeros_like(total)
    quarter = 4 * WIDTH

    def add(ch, source):
        info = side[ch, source]
        v = got1[ch, source].astype(F32)
        v = v * jnp.abs(v)
        high = v.astype(BF16)
        lower = (v - high.astype(F32)).astype(BF16)
        key = info[0:1, 0:CR]
        unit = info[1:2, 0:CR]
        for n in range(4):
            row = lax.broadcasted_iota(jnp.int32, (quarter, CR), 0).astype(F32) + float(n * quarter)
            pick = jnp.where(row == key, unit, 0.0).astype(BF16)
            total[n * quarter : (n + 1) * quarter, :] += jnp.dot(
                pick, high, preferred_element_type=F32
            ) + jnp.dot(pick, lower, preferred_element_type=F32)

    for ch in range(CHUNKS):
        add(ch, g)

        def take(p, carry, ch=ch):
            data, extra = piece(ch, p)
            extra.wait_recv()
            data.wait_recv()
            add(ch, lax.bitwise_xor(g, p))
            return carry

        lax.fori_loop(1, GRP, take, 0)

    def home(p):
        where = lax.bitwise_xor(g, p)
        return (
            remote(out2.at[where], got2.at[g], e_send.at[p], e_recv.at[p], {"grp": where}),
            remote(scale_out.at[where], scale2.at[g], f_send.at[p], f_recv.at[p], {"grp": where}),
        )

    def owned(where):
        value = total[pl.ds(pl.multiple_of(where * WIDTH, 16), WIDTH), :]
        most = jnp.max(jnp.max(jnp.abs(value), axis=1, keepdims=True), axis=0, keepdims=True)
        unit = jnp.maximum(most, 1e-25) * (1.004 / (FULL * FULL))
        return code(value, 1.0 / unit), jnp.broadcast_to(unit, (8, 128))

    got2[g], scale2[g] = owned(g)

    def give(p, carry):
        where = lax.bitwise_xor(g, p)
        out2[where], scale_out[where] = owned(where)
        data, extra = home(p)
        extra.start()
        data.start()
        return carry

    lax.fori_loop(1, GRP, give, 0)

    def place(m):
        v = got2[m].astype(F32)
        v = v * jnp.abs(v) * scale2[m][0:1, 0:1]
        for h in range(2):
            flat = v[:, 128 * h : 128 * h + 128].T
            result[2 * GRP * h + m] = flat[0:B]
            result[2 * GRP * h + GRP + m] = flat[B : 2 * B]

    place(g)

    def finish(p, carry):
        data, extra = home(p)
        extra.wait()
        data.wait()
        place(lax.bitwise_xor(g, p))
        for ch in range(CHUNKS):
            data, extra = piece(ch, p)
            extra.wait_send()
            data.wait_send()
        return carry

    lax.fori_loop(1, GRP, finish, 0)
    for copy in sends:
        copy.wait_send()
    near(0, GRP + s, {"slab": 1 - s}).wait_send()

    @pl.when(c < NCOL - 1)
    def _():
        near(1, GRP + 2, {"col": c + 1}).wait_send()

    @pl.when(c > 0)
    def _():
        near(2, GRP + 3, {"col": c - 1}).wait_send()


def per_device(fine_blocks, prolong, column_ids, aggregate_ids, live_rows):
    vmem = pl.BlockSpec(memory_space=pltpu.VMEM)
    smem = pl.BlockSpec(memory_space=pltpu.SMEM)
    dma = pltpu.SemaphoreType.DMA
    out = pl.pallas_call(
        kernel,
        out_shape=jax.ShapeDtypeStruct((B, B, WIDTH), F32),
        in_specs=[pl.BlockSpec(memory_space=pl.ANY), vmem, vmem, smem, smem, smem],
        out_specs=vmem,
        scratch_shapes=[
            pltpu.VMEM((RB, KA, B, B), BF16),
            pltpu.VMEM((GRP + 4, MSG, 128), BF16),
            pltpu.VMEM((2 * TILES, B, 128), BF16),
            pltpu.VMEM((RB, B, B), BF16),
            pltpu.VMEM((RB, KP // 2, 2 * B, 128), BF16),
            pltpu.VMEM((8, 128), jnp.int32),
            pltpu.VMEM((2 * GRP * CR, 128), F32),
            pltpu.VMEM((CHUNKS, GRP, CR, 256), jnp.int16),
            pltpu.VMEM((CHUNKS, GRP, CR, 256), jnp.int16),
            pltpu.VMEM((CHUNKS, 8, 128), F32),
            pltpu.VMEM((CHUNKS, GRP, 8, 128), F32),
            pltpu.VMEM((GRP * WIDTH, 256), F32),
            pltpu.VMEM((GRP, WIDTH, 256), jnp.int16),
            pltpu.VMEM((GRP, 8, 128), F32),
            pltpu.VMEM((GRP, WIDTH, 256), jnp.int16),
            pltpu.VMEM((GRP, 8, 128), F32),
            dma,
            dma((32,)),
            dma((32,)),
            dma((3,)),
            dma((3,)),
            dma((CHUNKS, GRP)),
            dma((CHUNKS, GRP)),
            dma((CHUNKS, GRP)),
            dma((CHUNKS, GRP)),
            dma((GRP,)),
            dma((GRP,)),
            dma((GRP,)),
            dma((GRP,)),
        ],
        compiler_params=pltpu.CompilerParams(
            collective_id=0, has_side_effects=True, vmem_limit_bytes=58 * 2**20
        ),
    )(fine_blocks, prolong, column_ids, column_ids, aggregate_ids, live_rows)
    return out.transpose(2, 0, 1)[None]


def solution(mesh):
    rows = ("slab", "grp", "col")
    return jax.shard_map(
        per_device,
        mesh=mesh,
        in_specs=(
            P(rows, None, None, None),
            P(rows, None, None),
            P(rows, None),
            P(rows),
            P(rows),
        ),
        out_specs=P(rows, None, None, None),
        check_vma=False,
    )
```

```python
import functools

import jax
import jax.numpy as jnp
from jax import lax
from jax.experimental import pallas as pl
from jax.experimental.pallas import tpu as pltpu
from jax.sharding import PartitionSpec as P

MESH = pl.DeviceIdType.MESH
GRP, SIDE, NCOL = 16, 4, 8
RB, KA, B = 8, 27, 64
KP = 28
CHUNKS, PER = 2, 4
CR = KP * PER
WIDTH = 80
TILES = 160
ORDER = (0, 10, 6, 9, 11, 14, 2, 5, 7, 8, 13, 15, 1, 3, 4, 12)
LAG = 3
BATCH = 4
MSG = 272
HALF = (pl.ds(0, 144), pl.ds(144, 128))
FULL = 32760.0
F32, BF16 = jnp.float32, jnp.bfloat16


def root(x, inverse):
    t = x * inverse
    return t * lax.rsqrt(jnp.maximum(jnp.abs(t), 1e-30))


def short(y):
    return y.astype(jnp.int32).astype(jnp.int16)


def decode(v):
    v = v.astype(F32)
    return v * (jnp.abs(v) + 1.0)


def remote(src, dst, send, recv, where):
    return pltpu.make_async_remote_copy(
        src_ref=src, dst_ref=dst, send_sem=send, recv_sem=recv, device_id=where, device_id_type=MESH
    )


def kernel(
    blocks_hbm, prolong_hbm, ids_hbm, ids, aggs, live,
    got2, scale2,
    prolong, ids_vec, pick, high, lower, blocks, tiles, table, flipped, u, ids_row, stage, out1, got1, keys, total, out2, scale_out,
    tile_sem, ids_sem, block_sem, ag_send, ag_recv, near_send, near_recv,
    d_send, d_recv, e_send, e_recv, f_send, f_recv,
):
    s, g, c = lax.axis_index("slab"), lax.axis_index("grp"), lax.axis_index("col")
    gy, gx = g // SIDE, lax.rem(g, SIDE)
    bar = pltpu.get_barrier_semaphore()
    for p in range(1, GRP):
        pl.semaphore_signal(bar, inc=1, device_id={"grp": lax.rem(g + p, GRP)}, device_id_type=MESH)
    pl.semaphore_signal(bar, inc=1, device_id={"slab": 1 - s}, device_id_type=MESH)

    @pl.when(c > 0)
    def _():
        pl.semaphore_signal(bar, inc=1, device_id={"col": c - 1}, device_id_type=MESH)

    @pl.when(c < NCOL - 1)
    def _():
        pl.semaphore_signal(bar, inc=1, device_id={"col": c + 1}, device_id_type=MESH)

    tile_copy = pltpu.make_async_copy(prolong_hbm, prolong, tile_sem)
    tile_copy.start()

    def block_copy(i):
        return pltpu.make_async_copy(blocks_hbm.at[i], blocks.at[i], block_sem.at[i])

    for i in range(RB):
        block_copy(i).start()
    ids_copy = pltpu.make_async_copy(ids_hbm, ids_vec, ids_sem)
    ids_copy.start()
    tile_copy.wait()

    alive = jnp.full((B, B), live[0], jnp.int32)
    for r in range(0, RB, 2):
        left, right = (
            jnp.where(alive > r + d, prolong[r + d].astype(F32), 0.0) for d in range(2)
        )
        tiles[g, 32 * r : 32 * r + B, :] = jnp.concatenate([left, right], axis=1).astype(BF16)
        flipped[r] = left.T.astype(BF16)
        flipped[r + 1] = right.T.astype(BF16)
    sub16 = lax.broadcasted_iota(jnp.int32, (16, 128), 0)
    agg_rows = jnp.zeros((16, 128), F32)
    for r in range(RB):
        agg_rows = jnp.where(sub16 == r, aggs[r].astype(F32), agg_rows)
    tiles[g, 256:MSG, :] = agg_rows.astype(BF16)

    tiles[GRP + s] = jnp.zeros((MSG, 128), BF16)

    @pl.when(c == 0)
    def _():
        tiles[GRP + 2] = jnp.zeros((MSG, 128), BF16)

    @pl.when(c == NCOL - 1)
    def _():
        tiles[GRP + 3] = jnp.zeros((MSG, 128), BF16)

    def u_row(i, carry):
        block_copy(i).wait()
        for k in range(0, KP, 2):
            left = jnp.dot(flipped[i], blocks[i, k], preferred_element_type=F32)
            if k + 1 < KA:
                right = jnp.dot(flipped[i], blocks[i, k + 1], preferred_element_type=F32)
            else:
                right = jnp.zeros((B, B), F32)
            value = jnp.concatenate([left, right], axis=1)
            high = value.astype(BF16)
            u[i, k // 2, 0:B, :] = high
            u[i, k // 2, B : 2 * B, :] = (value - high.astype(F32)).astype(BF16)
        return carry

    u_row(0, 0)
    cols = (c + NCOL - 1) // NCOL + (2 * NCOL - 2 - c) // NCOL
    pl.semaphore_wait(bar, GRP + cols)

    sends = []

    def spread(slot, half, y, x, source):
        copy = remote(
            tiles.at[slot, HALF[half]],
            tiles.at[slot, HALF[half]],
            ag_send.at[len(sends)],
            ag_recv.at[source * 2 + half],
            {"grp": y * SIDE + x},
        )
        copy.start()
        sends.append(copy)

    def arrived(dy, dx, half):
        slot = lax.rem(gy + dy, SIDE) * SIDE + lax.rem(gx + dx, SIDE)
        remote(
            tiles.at[slot, HALF[half]], tiles.at[slot, HALF[half]],
            ag_send.at[0], ag_recv.at[(dy * SIDE + dx) * 2 + half], {"grp": lax.rem(g + 1, GRP)},
        ).wait_recv()
        return slot

    for d in (1, 3, 2):
        back = SIDE - d
        spread(g, 0, gy, lax.rem(gx + d, SIDE), back)
        spread(g, 1, lax.rem(gy + d, SIDE), gx, back * SIDE)
    for d in (1, 3, 2):
        back = SIDE - d
        spread(g, 1, gy, lax.rem(gx + d, SIDE), back)
        spread(g, 0, lax.rem(gy + d, SIDE), gx, back * SIDE)

    def near(k, slot, where):
        return remote(tiles.at[g], tiles.at[slot], near_send.at[k], near_recv.at[k], where)

    near(0, GRP + s, {"slab": 1 - s}).start()

    @pl.when(c < NCOL - 1)
    def _():
        near(1, GRP + 2, {"col": c + 1}).start()

    @pl.when(c > 0)
    def _():
        near(2, GRP + 3, {"col": c - 1}).start()

    wide = lax.broadcasted_iota(jnp.int32, (B, 128), 1) < B

    def unfold(slot):
        def pair(n, carry):
            both = tiles[slot, pl.ds(pl.multiple_of(n * B, B), B), :].astype(F32)
            turned = pltpu.roll(both, B, 1)
            at = slot * RB + 2 * n
            table[at] = jnp.where(wide, both, 0.0).astype(BF16)
            table[at + 1] = jnp.where(wide, turned, 0.0).astype(BF16)
            table[TILES + at] = jnp.where(wide, 0.0, turned).astype(BF16)
            table[TILES + at + 1] = jnp.where(wide, 0.0, both).astype(BF16)
            return carry

        lax.fori_loop(0, RB // 2, pair, 0)

    for n, e in enumerate((1, 3, 2)):
        lax.fori_loop(1 + n, 2 + n, u_row, 0)
        slot = arrived(0, e, 0)
        for d in (1, 3, 2):
            spread(slot, 0, lax.rem(gy + d, SIDE), gx, (SIDE - d) * SIDE + e)
        slot = arrived(e, 0, 1)
        for d in (1, 3, 2):
            spread(slot, 1, gy, lax.rem(gx + d, SIDE), e * SIDE + SIDE - d)

    lax.fori_loop(4, RB, u_row, 0)
    unfold(g)
    for e in (1, 3, 2):
        unfold(arrived(0, e, 1))
        unfold(arrived(e, 0, 0))
    near(0, GRP + 1 - s, {"slab": 1 - s}).wait_recv()

    @pl.when(c > 0)
    def _():
        near(1, GRP + 2, {"col": c - 1}).wait_recv()

    @pl.when(c < NCOL - 1)
    def _():
        near(2, GRP + 3, {"col": c + 1}).wait_recv()

    for slot in range(GRP, GRP + 4):
        unfold(slot)
    for e in (1, 3, 2):
        for f in (1, 3, 2):
            arrived(e, f, 0)
            unfold(arrived(e, f, 1))

    ids_copy.wait()
    ids_row[...] = jnp.full((8, 128), -1, jnp.int32)
    ids_row[:, 0:KA] = ids_vec[...]
    lane = lax.broadcasted_iota(jnp.int32, (8, 128), 1)
    sub = lax.broadcasted_iota(jnp.int32, (8, 128), 0)
    for ch in range(CHUNKS):
        q = jnp.full((8, 128), -1, jnp.int32)
        owner = jnp.zeros((8, 128), F32)
        for ii in range(PER):
            i = PER * ch + ii
            row = jnp.broadcast_to(ids_row[i : i + 1, :], (8, 128))
            inside = (lane >= KP * ii) & (lane < KP * (ii + 1))
            q = jnp.where(inside, pltpu.roll(row, KP * ii, 1) if ii else row, q)
            owner = jnp.where(inside, aggs[i].astype(F32), owner)
        slot = jnp.zeros((8, 128), F32)
        for d in range(GRP + 4):
            base = 0 if d < GRP else (d - GRP + 1) * GRP
            named = tiles[d, 256:MSG, :].astype(F32)[0:8]
            slot = slot + jnp.where(q == sub + 8 * d, named + base, 0.0)
        slot = jnp.broadcast_to(jnp.sum(slot, axis=0, keepdims=True), (8, 128))
        key = jnp.where(q < 0, -1.0, owner * WIDTH + slot)
        keys[ch] = key

    low = lax.broadcasted_iota(jnp.int32, (8, 128), 1) < B

    def piece(ch, p):
        where = lax.bitwise_xor(g, p)
        return remote(out1.at[ch, where], got1.at[ch, g], d_send.at[ch, p], d_recv.at[ch, p], {"grp": where})

    high[...] = jnp.zeros_like(high)
    lower[...] = jnp.zeros_like(lower)
    pick[...] = jnp.zeros_like(pick)

    def load(ch, n, source):
        v = decode(got1[ch, source])
        top = v.astype(BF16)
        high[n * 128 : n * 128 + CR, :] = top
        lower[n * 128 : n * 128 + CR, :] = (v - top.astype(F32)).astype(BF16)
        key = got1[ch, source, 16:32, 0:128].astype(F32)[KP - 17 : KP - 16, 0:CR]
        unit = jnp.exp2(got1[ch, source, 48:64, 0:128].astype(F32)[2 * KP - 49 : 2 * KP - 48, 0:CR])
        for r in range(0, GRP * WIDTH, 64):
            row = lax.broadcasted_iota(jnp.int32, (64, CR), 0).astype(F32) + float(r)
            pick[r : r + 64, n * 128 : n * 128 + CR] = jnp.where(row == key, unit, 0.0).astype(BF16)

    def batch(ch, first, count):
        for n in range(count):
            p = ORDER[first + n]
            if p:
                piece(ch, p).wait_recv()
            load(ch, n, lax.bitwise_xor(g, p))
        depth = 128 * count
        value = jnp.dot(pick[:, 0:depth], high[0:depth, :], preferred_element_type=F32)
        value = value + jnp.dot(pick[:, 0:depth], lower[0:depth, :], preferred_element_type=F32)
        if ch or first:
            total[...] += value
        else:
            total[...] = value

    row_of = lax.broadcasted_iota(jnp.int32, (CR, 128), 0)
    for ch in range(CHUNKS):
        def t_row(ii, scales, ch=ch):
            i = PER * ch + ii
            top = jnp.zeros((8, 128), F32)
            for k in range(0, KP, 2):
                weights = jnp.concatenate(
                    [table[ids[i, k]], table[TILES + ids[i, min(k + 1, KA - 1)]]], axis=0
                )
                both = jnp.dot(u[i, k // 2], weights, preferred_element_type=F32)
                value = both[0:B] + both[B : 2 * B]
                top = jnp.maximum(top, jnp.max(jnp.abs(value).reshape(8, 8, 128), axis=0))
                for half in range(2):
                    for w in range(2):
                        first = value[32 * w + 8 * half : 32 * w + 8 * half + 8]
                        second = value[32 * w + 16 + 8 * half : 32 * w + 24 + 8 * half]
                        at = CR * (GRP * w + 8 * half) + KP * ii + k
                        stage[pl.ds(at, 8, stride=CR), :] = jnp.where(low, first, pltpu.roll(second, B, 1))
                        stage[pl.ds(at + 1, 8, stride=CR), :] = jnp.where(low, pltpu.roll(first, B, 1), second)
            most = jnp.max(jnp.max(top, axis=1, keepdims=True), axis=0, keepdims=True)
            most = jnp.broadcast_to(most, (8, 128))
            power = jnp.ceil(jnp.log2(jnp.maximum(most, 1e-25) * (1.004 / (FULL * FULL))))
            return tuple(jnp.where(ii == n, power, scales[n]) for n in range(PER))

        scales = lax.fori_loop(0, PER, t_row, tuple(jnp.zeros((8, 128), F32) for _ in range(PER)))
        powers = jnp.zeros((8, 128), F32)
        inverse = jnp.zeros((CR, 128), F32)
        for ii in range(PER):
            powers = jnp.where((lane >= KP * ii) & (lane < KP * (ii + 1)), scales[ii], powers)
            inverse = jnp.where(row_of >= KP * ii, jnp.exp2(-scales[ii])[0:1], inverse)

        def coded(where, ch=ch, inverse=inverse, powers=powers):
            first = root(stage[pl.ds(pl.multiple_of(where * CR, 16), CR), :], inverse)
            second = root(stage[pl.ds(pl.multiple_of((GRP + where) * CR, 16), CR), :], inverse)
            first = jnp.where(row_of == KP - 1, keys[ch][0:1], first)
            first = jnp.where(row_of == 2 * KP - 1, powers[0:1], first)
            return jnp.concatenate([short(first), short(second)], axis=1)

        got1[ch, g] = coded(g)
        for n in range(1, GRP):
            p = ORDER[n]
            where = lax.bitwise_xor(g, p)
            out1[ch, where] = coded(where)
            if ch and n > LAG:
                piece(0, ORDER[n - LAG]).wait_send()
            piece(ch, p).start()
            if ch and n % BATCH == BATCH - 1:
                batch(0, n - BATCH + 1, BATCH)

    batch(1, 0, 4)
    batch(1, 4, 4)
    batch(1, 8, 4)
    batch(1, 12, 2)
    batch(1, 14, 2)

    def home(p):
        where = lax.bitwise_xor(g, p)
        return (
            remote(out2.at[where], got2.at[g], e_send.at[p], e_recv.at[p], {"grp": where}),
            remote(scale_out.at[where], scale2.at[g], f_send.at[p], f_recv.at[p], {"grp": where}),
        )

    def owned(where):
        value = total[pl.ds(pl.multiple_of(where * WIDTH, 16), WIDTH), :]
        most = jnp.max(jnp.max(jnp.abs(value), axis=1, keepdims=True), axis=0, keepdims=True)
        unit = jnp.maximum(most, 1e-25) * (1.004 / (FULL * FULL))
        return short(root(value, 1.0 / unit)), jnp.broadcast_to(unit, (8, 128))

    got2[g], scale2[g] = owned(g)

    for p in ORDER[1:]:
        where = lax.bitwise_xor(g, p)
        out2[where], scale_out[where] = owned(where)
        for copy in home(p):
            copy.start()

    for p in ORDER[1:]:
        for copy in home(p):
            copy.wait()
        piece(1, p).wait_send()
    for p in ORDER[GRP - LAG :]:
        piece(0, p).wait_send()
    for copy in sends:
        copy.wait_send()
    near(0, GRP + s, {"slab": 1 - s}).wait_send()

    @pl.when(c < NCOL - 1)
    def _():
        near(1, GRP + 2, {"col": c + 1}).wait_send()

    @pl.when(c > 0)
    def _():
        near(2, GRP + 3, {"col": c - 1}).wait_send()


def unpack(got, scale, out):
    for m in range(GRP):
        v = decode(got[m]) * scale[m][0:1, 0:1]
        flat = v.T
        for h in range(2):
            out[GRP * h + m] = flat[B * h : B * (h + 1), :]


def per_device(fine_blocks, prolong, column_ids, aggregate_ids, live_rows):
    vmem = pl.BlockSpec(memory_space=pltpu.VMEM)
    hbm = pl.BlockSpec(memory_space=pltpu.HBM)
    smem = pl.BlockSpec(memory_space=pltpu.SMEM)
    dma = pltpu.SemaphoreType.DMA
    coded, scale = pl.pallas_call(
        kernel,
        out_shape=[
            jax.ShapeDtypeStruct((GRP, WIDTH, 256), jnp.int16),
            jax.ShapeDtypeStruct((GRP, 8, 128), F32),
        ],
        in_specs=[hbm, hbm, hbm, smem, smem, smem],
        out_specs=[vmem, vmem],
        scratch_shapes=[
            pltpu.VMEM((RB, B, B), BF16),
            pltpu.VMEM((RB, KA), jnp.int32),
            pltpu.VMEM((GRP * WIDTH, BATCH * 128), BF16),
            pltpu.VMEM((BATCH * 128, 256), BF16),
            pltpu.VMEM((BATCH * 128, 256), BF16),
            pltpu.VMEM((RB, KA, B, B), BF16),
            pltpu.VMEM((GRP + 4, MSG, 128), BF16),
            pltpu.VMEM((2 * TILES, B, 128), BF16),
            pltpu.VMEM((RB, B, B), BF16),
            pltpu.VMEM((RB, KP // 2, 2 * B, 128), BF16),
            pltpu.VMEM((8, 128), jnp.int32),
            pltpu.VMEM((2 * GRP * CR, 128), F32),
            pltpu.VMEM((CHUNKS, GRP, CR, 256), jnp.int16),
            pltpu.VMEM((CHUNKS, GRP, CR, 256), jnp.int16),
            pltpu.VMEM((CHUNKS, 8, 128), F32),
            pltpu.VMEM((GRP * WIDTH, 256), F32),
            pltpu.VMEM((GRP, WIDTH, 256), jnp.int16),
            pltpu.VMEM((GRP, 8, 128), F32),
            dma,
            dma,
            dma((RB,)),
            dma((32,)),
            dma((32,)),
            dma((3,)),
            dma((3,)),
            dma((CHUNKS, GRP)),
            dma((CHUNKS, GRP)),
            dma((GRP,)),
            dma((GRP,)),
            dma((GRP,)),
            dma((GRP,)),
        ],
        compiler_params=pltpu.CompilerParams(
            collective_id=0, has_side_effects=True, vmem_limit_bytes=58 * 2**20
        ),
    )(fine_blocks, prolong, column_ids, column_ids, aggregate_ids, live_rows)
    out = pl.pallas_call(
        unpack,
        grid=(2,),
        out_shape=jax.ShapeDtypeStruct((B, B, WIDTH), F32),
        in_specs=[
            pl.BlockSpec((GRP, WIDTH, 128), lambda j: (0, 0, j)),
            pl.BlockSpec((GRP, 8, 128), lambda j: (0, 0, 0)),
        ],
        out_specs=pl.BlockSpec((2 * GRP, B, WIDTH), lambda j: (j, 0, 0)),
        compiler_params=pltpu.CompilerParams(vmem_limit_bytes=58 * 2**20),
    )(coded, scale)
    return out.transpose(2, 0, 1)[None]


def solution(mesh):
    rows = ("slab", "grp", "col")
    return jax.shard_map(
        per_device,
        mesh=mesh,
        in_specs=(
            P(rows, None, None, None),
            P(rows, None, None),
            P(rows, None),
            P(rows),
            P(rows),
        ),
        out_specs=P(rows, None, None, None),
        check_vma=False,
    )
```

```python
import functools

import jax
import jax.numpy as jnp
from jax import lax
from jax.experimental import pallas as pl
from jax.experimental.pallas import tpu as pltpu
from jax.sharding import PartitionSpec as P

MESH = pl.DeviceIdType.MESH
GRP, SIDE, NCOL = 16, 4, 8
RB, KA, B = 8, 27, 64
KP = 28
CHUNKS, PER = 2, 4
CR = KP * PER
WIDTH = 80
TILES = 160
EARLY = 2
ORDER = (0, 10, 6, 9, 11, 14, 2, 5, 7, 8, 13, 15, 1, 3, 4, 12)
LAG = 3
BATCH = 4
MSG = 272
HALF = (pl.ds(0, 144), pl.ds(144, 128))
FULL = 32760.0
F32, BF16 = jnp.float32, jnp.bfloat16


def root(x, inverse):
    t = x * inverse
    return t * lax.rsqrt(jnp.maximum(jnp.abs(t), 1e-30))


def short(y):
    return y.astype(jnp.int32).astype(jnp.int16)


def decode(v):
    v = v.astype(F32)
    return v * (jnp.abs(v) + 1.0)


def remote(src, dst, send, recv, where):
    return pltpu.make_async_remote_copy(
        src_ref=src, dst_ref=dst, send_sem=send, recv_sem=recv, device_id=where, device_id_type=MESH
    )


def kernel(
    blocks_hbm, prolong_hbm, ids_hbm, aggs_hbm, live_hbm,
    got2, scale2,
    prolong, ids_vec, ids, aggs, live, pick, high, lower, blocks, tiles, table, flipped, u, ids_row, stage, out1, got1, keys, total, out2, scale_out,
    small_sem, block_sem, ag_send, ag_recv, near_send, near_recv,
    d_send, d_recv, e_send, e_recv, f_send, f_recv,
):
    s, g, c = lax.axis_index("slab"), lax.axis_index("grp"), lax.axis_index("col")
    gy, gx = g // SIDE, lax.rem(g, SIDE)
    bar = pltpu.get_barrier_semaphore()
    for p in range(1, GRP):
        pl.semaphore_signal(bar, inc=1, device_id={"grp": lax.rem(g + p, GRP)}, device_id_type=MESH)
    pl.semaphore_signal(bar, inc=1, device_id={"slab": 1 - s}, device_id_type=MESH)

    @pl.when(c > 0)
    def _():
        pl.semaphore_signal(bar, inc=1, device_id={"col": c - 1}, device_id_type=MESH)

    @pl.when(c < NCOL - 1)
    def _():
        pl.semaphore_signal(bar, inc=1, device_id={"col": c + 1}, device_id_type=MESH)

    small = [
        pltpu.make_async_copy(src, dst, small_sem.at[n])
        for n, (src, dst) in enumerate(
            ((prolong_hbm, prolong), (live_hbm, live), (aggs_hbm, aggs), (ids_hbm, ids_vec), (ids_hbm, ids))
        )
    ]
    for copy in small:
        copy.start()

    def block_copy(i):
        return pltpu.make_async_copy(blocks_hbm.at[i], blocks.at[i], block_sem.at[i])

    for i in range(RB):
        block_copy(i).start()
    for copy in small[:3]:
        copy.wait()

    alive = jnp.full((B, B), live[0], jnp.int32)
    for r in range(0, RB, 2):
        left, right = (
            jnp.where(alive > r + d, prolong[r + d].astype(F32), 0.0) for d in range(2)
        )
        tiles[g, 32 * r : 32 * r + B, :] = jnp.concatenate([left, right], axis=1).astype(BF16)
        flipped[r] = left.T.astype(BF16)
        flipped[r + 1] = right.T.astype(BF16)
    sub16 = lax.broadcasted_iota(jnp.int32, (16, 128), 0)
    agg_rows = jnp.zeros((16, 128), F32)
    for r in range(RB):
        agg_rows = jnp.where(sub16 == r, aggs[r].astype(F32), agg_rows)
    tiles[g, 256:MSG, :] = agg_rows.astype(BF16)

    tiles[GRP + s] = jnp.zeros((MSG, 128), BF16)

    @pl.when(c == 0)
    def _():
        tiles[GRP + 2] = jnp.zeros((MSG, 128), BF16)

    @pl.when(c == NCOL - 1)
    def _():
        tiles[GRP + 3] = jnp.zeros((MSG, 128), BF16)

    def u_row(i, carry):
        block_copy(i).wait()
        for k in range(0, KP, 2):
            left = jnp.dot(flipped[i], blocks[i, k], preferred_element_type=F32)
            if k + 1 < KA:
                right = jnp.dot(flipped[i], blocks[i, k + 1], preferred_element_type=F32)
            else:
                right = jnp.zeros((B, B), F32)
            value = jnp.concatenate([left, right], axis=1)
            high = value.astype(BF16)
            u[i, k // 2, 0:B, :] = high
            u[i, k // 2, B : 2 * B, :] = (value - high.astype(F32)).astype(BF16)
        return carry

    lax.fori_loop(0, EARLY, u_row, 0)
    cols = (c + NCOL - 1) // NCOL + (2 * NCOL - 2 - c) // NCOL
    pl.semaphore_wait(bar, GRP + cols)

    sends = []

    def spread(slot, half, y, x, source):
        copy = remote(
            tiles.at[slot, HALF[half]],
            tiles.at[slot, HALF[half]],
            ag_send.at[len(sends)],
            ag_recv.at[source * 2 + half],
            {"grp": y * SIDE + x},
        )
        copy.start()
        sends.append(copy)

    def arrived(dy, dx, half):
        slot = lax.rem(gy + dy, SIDE) * SIDE + lax.rem(gx + dx, SIDE)
        remote(
            tiles.at[slot, HALF[half]], tiles.at[slot, HALF[half]],
            ag_send.at[0], ag_recv.at[(dy * SIDE + dx) * 2 + half], {"grp": lax.rem(g + 1, GRP)},
        ).wait_recv()
        return slot

    for d in (1, 3, 2):
        back = SIDE - d
        spread(g, 0, gy, lax.rem(gx + d, SIDE), back)
        spread(g, 1, lax.rem(gy + d, SIDE), gx, back * SIDE)
    for d in (1, 3, 2):
        back = SIDE - d
        spread(g, 1, gy, lax.rem(gx + d, SIDE), back)
        spread(g, 0, lax.rem(gy + d, SIDE), gx, back * SIDE)

    def near(k, slot, where):
        return remote(tiles.at[g], tiles.at[slot], near_send.at[k], near_recv.at[k], where)

    near(0, GRP + s, {"slab": 1 - s}).start()

    @pl.when(c < NCOL - 1)
    def _():
        near(1, GRP + 2, {"col": c + 1}).start()

    @pl.when(c > 0)
    def _():
        near(2, GRP + 3, {"col": c - 1}).start()

    wide = lax.broadcasted_iota(jnp.int32, (B, 128), 1) < B
    first_half = jnp.where(wide, 1.0, 0.0).astype(BF16)
    second_half = jnp.where(wide, 0.0, 1.0).astype(BF16)

    def unfold(slot):
        def pair(n, carry):
            both = tiles[slot, pl.ds(pl.multiple_of(n * B, B), B), :]
            turned = pltpu.roll(both.astype(F32), B, 1).astype(BF16)
            at = slot * RB + 2 * n
            table[at] = both * first_half
            table[at + 1] = turned * first_half
            table[TILES + at] = turned * second_half
            table[TILES + at + 1] = both * second_half
            return carry

        lax.fori_loop(0, RB // 2, pair, 0)

    for n, e in enumerate((1, 3, 2)):
        lax.fori_loop(EARLY + n, EARLY + n + 1, u_row, 0)
        slot = arrived(0, e, 0)
        for d in (1, 3, 2):
            spread(slot, 0, lax.rem(gy + d, SIDE), gx, (SIDE - d) * SIDE + e)
        slot = arrived(e, 0, 1)
        for d in (1, 3, 2):
            spread(slot, 1, gy, lax.rem(gx + d, SIDE), e * SIDE + SIDE - d)

    lax.fori_loop(EARLY + 3, RB, u_row, 0)
    unfold(g)
    for e in (1, 3, 2):
        unfold(arrived(0, e, 1))
        unfold(arrived(e, 0, 0))
    near(0, GRP + 1 - s, {"slab": 1 - s}).wait_recv()

    @pl.when(c > 0)
    def _():
        near(1, GRP + 2, {"col": c - 1}).wait_recv()

    @pl.when(c < NCOL - 1)
    def _():
        near(2, GRP + 3, {"col": c + 1}).wait_recv()

    for slot in range(GRP, GRP + 4):
        unfold(slot)
    for e in (1, 3, 2):
        for f in (1, 3, 2):
            arrived(e, f, 0)
            unfold(arrived(e, f, 1))

    for copy in small[3:]:
        copy.wait()
    ids_row[...] = jnp.full((8, 128), -1, jnp.int32)
    ids_row[:, 0:KA] = ids_vec[...]
    lane = lax.broadcasted_iota(jnp.int32, (8, 128), 1)
    sub = lax.broadcasted_iota(jnp.int32, (8, 128), 0)
    for ch in range(CHUNKS):
        q = jnp.full((8, 128), -1, jnp.int32)
        owner = jnp.zeros((8, 128), F32)
        for ii in range(PER):
            i = PER * ch + ii
            row = jnp.broadcast_to(ids_row[i : i + 1, :], (8, 128))
            inside = (lane >= KP * ii) & (lane < KP * (ii + 1))
            q = jnp.where(inside, pltpu.roll(row, KP * ii, 1) if ii else row, q)
            owner = jnp.where(inside, aggs[i].astype(F32), owner)
        slot = jnp.zeros((8, 128), F32)
        for d in range(GRP + 4):
            base = 0 if d < GRP else (d - GRP + 1) * GRP
            named = tiles[d, 256:MSG, :].astype(F32)[0:8]
            slot = slot + jnp.where(q == sub + 8 * d, named + base, 0.0)
        slot = jnp.broadcast_to(jnp.sum(slot, axis=0, keepdims=True), (8, 128))
        key = jnp.where(q < 0, -1.0, owner * WIDTH + slot)
        keys[ch] = key

    low = lax.broadcasted_iota(jnp.int32, (8, 128), 1) < B

    def piece(ch, p):
        where = lax.bitwise_xor(g, p)
        return remote(out1.at[ch, where], got1.at[ch, g], d_send.at[ch, p], d_recv.at[ch, p], {"grp": where})

    high[...] = jnp.zeros_like(high)
    lower[...] = jnp.zeros_like(lower)
    pick[...] = jnp.zeros_like(pick)

    def load(ch, n, source):
        v = decode(got1[ch, source])
        top = v.astype(BF16)
        high[n * 128 : n * 128 + CR, :] = top
        lower[n * 128 : n * 128 + CR, :] = (v - top.astype(F32)).astype(BF16)
        key = got1[ch, source, 16:32, 0:128].astype(F32)[KP - 17 : KP - 16, 0:CR]
        unit = jnp.exp2(got1[ch, source, 48:64, 0:128].astype(F32)[2 * KP - 49 : 2 * KP - 48, 0:CR])
        for r in range(0, GRP * WIDTH, 64):
            row = lax.broadcasted_iota(jnp.int32, (64, CR), 0).astype(F32) + float(r)
            pick[r : r + 64, n * 128 : n * 128 + CR] = jnp.where(row == key, unit, 0.0).astype(BF16)

    def batch(ch, first, count):
        for n in range(count):
            p = ORDER[first + n]
            if p:
                piece(ch, p).wait_recv()
            load(ch, n, lax.bitwise_xor(g, p))
        depth = 128 * count
        value = jnp.dot(pick[:, 0:depth], high[0:depth, :], preferred_element_type=F32)
        value = value + jnp.dot(pick[:, 0:depth], lower[0:depth, :], preferred_element_type=F32)
        if ch or first:
            total[...] += value
        else:
            total[...] = value

    row_of = lax.broadcasted_iota(jnp.int32, (CR, 128), 0)
    for ch in range(CHUNKS):
        def t_row(ii, scales, ch=ch):
            i = PER * ch + ii
            top = jnp.zeros((8, 128), F32)
            for k in range(0, KP, 2):
                weights = jnp.concatenate(
                    [table[ids[i, k]], table[TILES + ids[i, min(k + 1, KA - 1)]]], axis=0
                )
                both = jnp.dot(u[i, k // 2], weights, preferred_element_type=F32)
                value = both[0:B] + both[B : 2 * B]
                top = jnp.maximum(top, jnp.max(jnp.abs(value).reshape(8, 8, 128), axis=0))
                for half in range(2):
                    for w in range(2):
                        first = value[32 * w + 8 * half : 32 * w + 8 * half + 8]
                        second = value[32 * w + 16 + 8 * half : 32 * w + 24 + 8 * half]
                        at = CR * (GRP * w + 8 * half) + KP * ii + k
                        stage[pl.ds(at, 8, stride=CR), :] = jnp.where(low, first, pltpu.roll(second, B, 1))
                        stage[pl.ds(at + 1, 8, stride=CR), :] = jnp.where(low, pltpu.roll(first, B, 1), second)
            most = jnp.max(jnp.max(top, axis=1, keepdims=True), axis=0, keepdims=True)
            most = jnp.broadcast_to(most, (8, 128))
            power = jnp.ceil(jnp.log2(jnp.maximum(most, 1e-25) * (1.004 / (FULL * FULL))))
            return tuple(jnp.where(ii == n, power, scales[n]) for n in range(PER))

        scales = lax.fori_loop(0, PER, t_row, tuple(jnp.zeros((8, 128), F32) for _ in range(PER)))
        powers = jnp.zeros((8, 128), F32)
        inverse = jnp.zeros((CR, 128), F32)
        for ii in range(PER):
            powers = jnp.where((lane >= KP * ii) & (lane < KP * (ii + 1)), scales[ii], powers)
            inverse = jnp.where(row_of >= KP * ii, jnp.exp2(-scales[ii])[0:1], inverse)

        def coded(where, ch=ch, inverse=inverse, powers=powers):
            first = root(stage[pl.ds(pl.multiple_of(where * CR, 16), CR), :], inverse)
            second = root(stage[pl.ds(pl.multiple_of((GRP + where) * CR, 16), CR), :], inverse)
            first = jnp.where(row_of == KP - 1, keys[ch][0:1], first)
            first = jnp.where(row_of == 2 * KP - 1, powers[0:1], first)
            return jnp.concatenate([short(first), short(second)], axis=1)

        got1[ch, g] = coded(g)
        for n in range(1, GRP):
            p = ORDER[n]
            where = lax.bitwise_xor(g, p)
            out1[ch, where] = coded(where)
            if ch and n > LAG:
                piece(0, ORDER[n - LAG]).wait_send()
            piece(ch, p).start()
            if ch and n % BATCH == BATCH - 1:
                batch(0, n - BATCH + 1, BATCH)

    batch(1, 0, 4)
    batch(1, 4, 4)
    batch(1, 8, 4)
    batch(1, 12, 2)
    batch(1, 14, 2)

    def home(p):
        where = lax.bitwise_xor(g, p)
        return (
            remote(out2.at[where], got2.at[g], e_send.at[p], e_recv.at[p], {"grp": where}),
            remote(scale_out.at[where], scale2.at[g], f_send.at[p], f_recv.at[p], {"grp": where}),
        )

    def owned(where):
        value = total[pl.ds(pl.multiple_of(where * WIDTH, 16), WIDTH), :]
        most = jnp.max(jnp.max(jnp.abs(value), axis=1, keepdims=True), axis=0, keepdims=True)
        unit = jnp.maximum(most, 1e-25) * (1.004 / (FULL * FULL))
        return short(root(value, 1.0 / unit)), jnp.broadcast_to(unit, (8, 128))

    got2[g], scale2[g] = owned(g)

    for p in ORDER[1:]:
        where = lax.bitwise_xor(g, p)
        out2[where], scale_out[where] = owned(where)
        for copy in home(p):
            copy.start()

    for p in ORDER[1:]:
        for copy in home(p):
            copy.wait()
        piece(1, p).wait_send()
    for p in ORDER[GRP - LAG :]:
        piece(0, p).wait_send()
    for copy in sends:
        copy.wait_send()
    near(0, GRP + s, {"slab": 1 - s}).wait_send()

    @pl.when(c < NCOL - 1)
    def _():
        near(1, GRP + 2, {"col": c + 1}).wait_send()

    @pl.when(c > 0)
    def _():
        near(2, GRP + 3, {"col": c - 1}).wait_send()


def unpack(got, scale, out):
    for m in range(GRP):
        v = decode(got[m]) * scale[m][0:1, 0:1]
        flat = v.T
        for h in range(2):
            out[GRP * h + m] = flat[B * h : B * (h + 1), :]


def per_device(fine_blocks, prolong, column_ids, aggregate_ids, live_rows):
    vmem = pl.BlockSpec(memory_space=pltpu.VMEM)
    hbm = pl.BlockSpec(memory_space=pltpu.HBM)
    dma = pltpu.SemaphoreType.DMA
    coded, scale = pl.pallas_call(
        kernel,
        out_shape=[
            jax.ShapeDtypeStruct((GRP, WIDTH, 256), jnp.int16),
            jax.ShapeDtypeStruct((GRP, 8, 128), F32),
        ],
        in_specs=[hbm] * 5,
        out_specs=[vmem, vmem],
        scratch_shapes=[
            pltpu.VMEM((RB, B, B), BF16),
            pltpu.VMEM((RB, KA), jnp.int32),
            pltpu.SMEM((RB, KA), jnp.int32),
            pltpu.SMEM((RB,), jnp.int32),
            pltpu.SMEM((1,), jnp.int32),
            pltpu.VMEM((GRP * WIDTH, BATCH * 128), BF16),
            pltpu.VMEM((BATCH * 128, 256), BF16),
            pltpu.VMEM((BATCH * 128, 256), BF16),
            pltpu.VMEM((RB, KA, B, B), BF16),
            pltpu.VMEM((GRP + 4, MSG, 128), BF16),
            pltpu.VMEM((2 * TILES, B, 128), BF16),
            pltpu.VMEM((RB, B, B), BF16),
            pltpu.VMEM((RB, KP // 2, 2 * B, 128), BF16),
            pltpu.VMEM((8, 128), jnp.int32),
            pltpu.VMEM((2 * GRP * CR, 128), F32),
            pltpu.VMEM((CHUNKS, GRP, CR, 256), jnp.int16),
            pltpu.VMEM((CHUNKS, GRP, CR, 256), jnp.int16),
            pltpu.VMEM((CHUNKS, 8, 128), F32),
            pltpu.VMEM((GRP * WIDTH, 256), F32),
            pltpu.VMEM((GRP, WIDTH, 256), jnp.int16),
            pltpu.VMEM((GRP, 8, 128), F32),
            dma((5,)),
            dma((RB,)),
            dma((32,)),
            dma((32,)),
            dma((3,)),
            dma((3,)),
            dma((CHUNKS, GRP)),
            dma((CHUNKS, GRP)),
            dma((GRP,)),
            dma((GRP,)),
            dma((GRP,)),
            dma((GRP,)),
        ],
        compiler_params=pltpu.CompilerParams(
            collective_id=0, has_side_effects=True, vmem_limit_bytes=58 * 2**20
        ),
    )(fine_blocks, prolong, column_ids, aggregate_ids, live_rows)
    out = pl.pallas_call(
        unpack,
        grid=(2,),
        out_shape=jax.ShapeDtypeStruct((B, B, WIDTH), F32),
        in_specs=[
            pl.BlockSpec((GRP, WIDTH, 128), lambda j: (0, 0, j)),
            pl.BlockSpec((GRP, 8, 128), lambda j: (0, 0, 0)),
        ],
        out_specs=pl.BlockSpec((2 * GRP, B, WIDTH), lambda j: (j, 0, 0)),
        compiler_params=pltpu.CompilerParams(vmem_limit_bytes=58 * 2**20),
    )(coded, scale)
    return out.transpose(2, 0, 1)[None]


def solution(mesh):
    rows = ("slab", "grp", "col")
    return jax.shard_map(
        per_device,
        mesh=mesh,
        in_specs=(
            P(rows, None, None, None),
            P(rows, None, None),
            P(rows, None),
            P(rows),
            P(rows),
        ),
        out_specs=P(rows, None, None, None),
        check_vma=False,
    )
```

```python
import functools

import jax
import jax.numpy as jnp
from jax import lax
from jax.experimental import pallas as pl
from jax.experimental.pallas import tpu as pltpu
from jax.sharding import PartitionSpec as P

MESH = pl.DeviceIdType.MESH
GRP, SIDE, NCOL = 16, 4, 8
RB, KA, B = 8, 27, 64
KP = 28
CHUNKS, PER = 2, 4
CR = KP * PER
WIDTH = 80
TILES = 160
EARLY = 4
ORDER = (0, 10, 6, 9, 11, 14, 2, 5, 7, 8, 13, 15, 1, 3, 4, 12)
LAG = 3
BATCH = 4
MSG = 272
HALF = (pl.ds(0, 144), pl.ds(144, 128))
FULL = 32760.0
F32, BF16 = jnp.float32, jnp.bfloat16


def root(x, inverse):
    t = x * inverse
    return t * lax.rsqrt(jnp.maximum(jnp.abs(t), 1e-30))


def short(y):
    return y.astype(jnp.int32).astype(jnp.int16)


def decode(v):
    v = v.astype(F32)
    return v * (jnp.abs(v) + 1.0)


def remote(src, dst, send, recv, where):
    return pltpu.make_async_remote_copy(
        src_ref=src, dst_ref=dst, send_sem=send, recv_sem=recv, device_id=where, device_id_type=MESH
    )


def kernel(
    blocks_hbm, prolong_hbm, ids_hbm, aggs_hbm, live_hbm,
    got2, scale2,
    prolong, ids_vec, ids, aggs, live, pick, high, lower, blocks, tiles, table, flipped, u, ids_row, stage, out1, got1, keys, total, out2, scale_out,
    small_sem, block_sem, ag_send, ag_recv, near_send, near_recv,
    d_send, d_recv, e_send, e_recv, f_send, f_recv,
):
    s, g, c = lax.axis_index("slab"), lax.axis_index("grp"), lax.axis_index("col")
    gy, gx = g // SIDE, lax.rem(g, SIDE)
    bar = pltpu.get_barrier_semaphore()
    for p in range(1, GRP):
        pl.semaphore_signal(bar, inc=1, device_id={"grp": lax.rem(g + p, GRP)}, device_id_type=MESH)
    pl.semaphore_signal(bar, inc=1, device_id={"slab": 1 - s}, device_id_type=MESH)

    @pl.when(c > 0)
    def _():
        pl.semaphore_signal(bar, inc=1, device_id={"col": c - 1}, device_id_type=MESH)

    @pl.when(c < NCOL - 1)
    def _():
        pl.semaphore_signal(bar, inc=1, device_id={"col": c + 1}, device_id_type=MESH)

    small = [
        pltpu.make_async_copy(src, dst, small_sem.at[n])
        for n, (src, dst) in enumerate(
            ((prolong_hbm, prolong), (live_hbm, live), (aggs_hbm, aggs), (ids_hbm, ids_vec), (ids_hbm, ids))
        )
    ]
    for copy in small:
        copy.start()

    def block_copy(i):
        return pltpu.make_async_copy(blocks_hbm.at[i], blocks.at[i], block_sem.at[i])

    for i in range(RB):
        block_copy(i).start()
    for copy in small[:3]:
        copy.wait()

    alive = jnp.full((B, B), live[0], jnp.int32)
    for r in range(0, RB, 2):
        left, right = (
            jnp.where(alive > r + d, prolong[r + d].astype(F32), 0.0) for d in range(2)
        )
        tiles[g, 32 * r : 32 * r + B, :] = jnp.concatenate([left, right], axis=1).astype(BF16)
        flipped[r] = left.T.astype(BF16)
        flipped[r + 1] = right.T.astype(BF16)
    sub16 = lax.broadcasted_iota(jnp.int32, (16, 128), 0)
    agg_rows = jnp.zeros((16, 128), F32)
    for r in range(RB):
        agg_rows = jnp.where(sub16 == r, aggs[r].astype(F32), agg_rows)
    tiles[g, 256:MSG, :] = agg_rows.astype(BF16)

    tiles[GRP + s] = jnp.zeros((MSG, 128), BF16)

    @pl.when(c == 0)
    def _():
        tiles[GRP + 2] = jnp.zeros((MSG, 128), BF16)

    @pl.when(c == NCOL - 1)
    def _():
        tiles[GRP + 3] = jnp.zeros((MSG, 128), BF16)

    def u_row(i, carry):
        block_copy(i).wait()
        for k in range(0, KP, 2):
            left = jnp.dot(flipped[i], blocks[i, k], preferred_element_type=F32)
            if k + 1 < KA:
                right = jnp.dot(flipped[i], blocks[i, k + 1], preferred_element_type=F32)
            else:
                right = jnp.zeros((B, B), F32)
            value = jnp.concatenate([left, right], axis=1)
            high = value.astype(BF16)
            u[i, k // 2, 0:B, :] = high
            u[i, k // 2, B : 2 * B, :] = (value - high.astype(F32)).astype(BF16)
        return carry

    lax.fori_loop(0, EARLY, u_row, 0)
    cols = (c + NCOL - 1) // NCOL + (2 * NCOL - 2 - c) // NCOL
    pl.semaphore_wait(bar, GRP + cols)

    sends = []

    def spread(slot, half, y, x, source):
        copy = remote(
            tiles.at[slot, HALF[half]],
            tiles.at[slot, HALF[half]],
            ag_send.at[len(sends)],
            ag_recv.at[source * 2 + half],
            {"grp": y * SIDE + x},
        )
        copy.start()
        sends.append(copy)

    def arrived(dy, dx, half):
        slot = lax.rem(gy + dy, SIDE) * SIDE + lax.rem(gx + dx, SIDE)
        remote(
            tiles.at[slot, HALF[half]], tiles.at[slot, HALF[half]],
            ag_send.at[0], ag_recv.at[(dy * SIDE + dx) * 2 + half], {"grp": lax.rem(g + 1, GRP)},
        ).wait_recv()
        return slot

    for d in (1, 3, 2):
        back = SIDE - d
        spread(g, 0, gy, lax.rem(gx + d, SIDE), back)
        spread(g, 1, lax.rem(gy + d, SIDE), gx, back * SIDE)
    for d in (1, 3, 2):
        back = SIDE - d
        spread(g, 1, gy, lax.rem(gx + d, SIDE), back)
        spread(g, 0, lax.rem(gy + d, SIDE), gx, back * SIDE)

    def near(k, slot, where):
        return remote(tiles.at[g], tiles.at[slot], near_send.at[k], near_recv.at[k], where)

    near(0, GRP + s, {"slab": 1 - s}).start()

    @pl.when(c < NCOL - 1)
    def _():
        near(1, GRP + 2, {"col": c + 1}).start()

    @pl.when(c > 0)
    def _():
        near(2, GRP + 3, {"col": c - 1}).start()

    wide = lax.broadcasted_iota(jnp.int32, (B, 128), 1) < B
    first_half = jnp.where(wide, 1.0, 0.0).astype(BF16)
    second_half = jnp.where(wide, 0.0, 1.0).astype(BF16)

    def unfold(slot):
        def pair(n, carry):
            both = tiles[slot, pl.ds(pl.multiple_of(n * B, B), B), :]
            turned = pltpu.roll(both.astype(F32), B, 1).astype(BF16)
            at = slot * RB + 2 * n
            table[at] = both * first_half
            table[at + 1] = turned * first_half
            table[TILES + at] = turned * second_half
            table[TILES + at + 1] = both * second_half
            return carry

        lax.fori_loop(0, RB // 2, pair, 0)

    for n, e in enumerate((1, 3, 2)):
        lax.fori_loop(EARLY + n, EARLY + n + 1, u_row, 0)
        slot = arrived(0, e, 0)
        for d in (1, 3, 2):
            spread(slot, 0, lax.rem(gy + d, SIDE), gx, (SIDE - d) * SIDE + e)
        slot = arrived(e, 0, 1)
        for d in (1, 3, 2):
            spread(slot, 1, gy, lax.rem(gx + d, SIDE), e * SIDE + SIDE - d)

    lax.fori_loop(EARLY + 3, RB, u_row, 0)
    unfold(g)
    for e in (1, 3, 2):
        unfold(arrived(0, e, 1))
        unfold(arrived(e, 0, 0))
    near(0, GRP + 1 - s, {"slab": 1 - s}).wait_recv()

    @pl.when(c > 0)
    def _():
        near(1, GRP + 2, {"col": c - 1}).wait_recv()

    @pl.when(c < NCOL - 1)
    def _():
        near(2, GRP + 3, {"col": c + 1}).wait_recv()

    for slot in range(GRP, GRP + 4):
        unfold(slot)
    for e in (1, 3, 2):
        for f in (1, 3, 2):
            arrived(e, f, 0)
            unfold(arrived(e, f, 1))

    for copy in small[3:]:
        copy.wait()
    ids_row[...] = jnp.full((8, 128), -1, jnp.int32)
    ids_row[:, 0:KA] = ids_vec[...]
    lane = lax.broadcasted_iota(jnp.int32, (8, 128), 1)
    sub = lax.broadcasted_iota(jnp.int32, (8, 128), 0)
    for ch in range(CHUNKS):
        q = jnp.full((8, 128), -1, jnp.int32)
        owner = jnp.zeros((8, 128), F32)
        for ii in range(PER):
            i = PER * ch + ii
            row = jnp.broadcast_to(ids_row[i : i + 1, :], (8, 128))
            inside = (lane >= KP * ii) & (lane < KP * (ii + 1))
            q = jnp.where(inside, pltpu.roll(row, KP * ii, 1) if ii else row, q)
            owner = jnp.where(inside, aggs[i].astype(F32), owner)
        slot = jnp.zeros((8, 128), F32)
        for d in range(GRP + 4):
            base = 0 if d < GRP else (d - GRP + 1) * GRP
            named = tiles[d, 256:MSG, :].astype(F32)[0:8]
            slot = slot + jnp.where(q == sub + 8 * d, named + base, 0.0)
        slot = jnp.broadcast_to(jnp.sum(slot, axis=0, keepdims=True), (8, 128))
        key = jnp.where(q < 0, -1.0, owner * WIDTH + slot)
        keys[ch] = key

    low = lax.broadcasted_iota(jnp.int32, (8, 128), 1) < B

    def piece(ch, p):
        where = lax.bitwise_xor(g, p)
        return remote(out1.at[ch, where], got1.at[ch, g], d_send.at[ch, p], d_recv.at[ch, p], {"grp": where})

    high[...] = jnp.zeros_like(high)
    lower[...] = jnp.zeros_like(lower)
    pick[...] = jnp.zeros_like(pick)

    def load(ch, n, source):
        v = decode(got1[ch, source])
        top = v.astype(BF16)
        high[n * 128 : n * 128 + CR, :] = top
        lower[n * 128 : n * 128 + CR, :] = (v - top.astype(F32)).astype(BF16)
        key = got1[ch, source, 16:32, 0:128].astype(F32)[KP - 17 : KP - 16, 0:CR]
        unit = jnp.exp2(got1[ch, source, 48:64, 0:128].astype(F32)[2 * KP - 49 : 2 * KP - 48, 0:CR])
        for r in range(0, GRP * WIDTH, 64):
            row = lax.broadcasted_iota(jnp.int32, (64, CR), 0).astype(F32) + float(r)
            pick[r : r + 64, n * 128 : n * 128 + CR] = jnp.where(row == key, unit, 0.0).astype(BF16)

    def batch(ch, first, count):
        for n in range(count):
            p = ORDER[first + n]
            if p:
                piece(ch, p).wait_recv()
            load(ch, n, lax.bitwise_xor(g, p))
        depth = 128 * count
        value = jnp.dot(pick[:, 0:depth], high[0:depth, :], preferred_element_type=F32)
        value = value + jnp.dot(pick[:, 0:depth], lower[0:depth, :], preferred_element_type=F32)
        if ch or first:
            total[...] += value
        else:
            total[...] = value

    row_of = lax.broadcasted_iota(jnp.int32, (CR, 128), 0)
    for ch in range(CHUNKS):
        def t_row(ii, scales, ch=ch):
            i = PER * ch + ii
            top = jnp.zeros((8, 128), F32)
            for k in range(0, KP, 2):
                weights = jnp.concatenate(
                    [table[ids[i, k]], table[TILES + ids[i, min(k + 1, KA - 1)]]], axis=0
                )
                both = jnp.dot(u[i, k // 2], weights, preferred_element_type=F32)
                value = both[0:B] + both[B : 2 * B]
                top = jnp.maximum(top, jnp.max(jnp.abs(value).reshape(8, 8, 128), axis=0))
                for half in range(2):
                    for w in range(2):
                        first = value[32 * w + 8 * half : 32 * w + 8 * half + 8]
                        second = value[32 * w + 16 + 8 * half : 32 * w + 24 + 8 * half]
                        at = CR * (GRP * w + 8 * half) + KP * ii + k
                        stage[pl.ds(at, 8, stride=CR), :] = jnp.where(low, first, pltpu.roll(second, B, 1))
                        stage[pl.ds(at + 1, 8, stride=CR), :] = jnp.where(low, pltpu.roll(first, B, 1), second)
            most = jnp.max(jnp.max(top, axis=1, keepdims=True), axis=0, keepdims=True)
            most = jnp.broadcast_to(most, (8, 128))
            power = jnp.ceil(jnp.log2(jnp.maximum(most, 1e-25) * (1.004 / (FULL * FULL))))
            return tuple(jnp.where(ii == n, power, scales[n]) for n in range(PER))

        scales = lax.fori_loop(0, PER, t_row, tuple(jnp.zeros((8, 128), F32) for _ in range(PER)))
        powers = jnp.zeros((8, 128), F32)
        inverse = jnp.zeros((CR, 128), F32)
        for ii in range(PER):
            powers = jnp.where((lane >= KP * ii) & (lane < KP * (ii + 1)), scales[ii], powers)
            inverse = jnp.where(row_of >= KP * ii, jnp.exp2(-scales[ii])[0:1], inverse)

        def coded(where, ch=ch, inverse=inverse, powers=powers):
            first = root(stage[pl.ds(pl.multiple_of(where * CR, 16), CR), :], inverse)
            second = root(stage[pl.ds(pl.multiple_of((GRP + where) * CR, 16), CR), :], inverse)
            first = jnp.where(row_of == KP - 1, keys[ch][0:1], first)
            first = jnp.where(row_of == 2 * KP - 1, powers[0:1], first)
            return jnp.concatenate([short(first), short(second)], axis=1)

        got1[ch, g] = coded(g)
        for n in range(1, GRP):
            p = ORDER[n]
            where = lax.bitwise_xor(g, p)
            out1[ch, where] = coded(where)
            if ch and n > LAG:
                piece(0, ORDER[n - LAG]).wait_send()
            piece(ch, p).start()
            if ch and n % BATCH == BATCH - 1:
                batch(0, n - BATCH + 1, BATCH)

    batch(1, 0, 4)
    batch(1, 4, 4)
    batch(1, 8, 4)
    batch(1, 12, 2)
    batch(1, 14, 2)

    def home(p):
        where = lax.bitwise_xor(g, p)
        return (
            remote(out2.at[where], got2.at[g], e_send.at[p], e_recv.at[p], {"grp": where}),
            remote(scale_out.at[where], scale2.at[g], f_send.at[p], f_recv.at[p], {"grp": where}),
        )

    def owned(where):
        value = total[pl.ds(pl.multiple_of(where * WIDTH, 16), WIDTH), :]
        most = jnp.max(jnp.max(jnp.abs(value), axis=1, keepdims=True), axis=0, keepdims=True)
        unit = jnp.maximum(most, 1e-25) * (1.004 / (FULL * FULL))
        return short(root(value, 1.0 / unit)), jnp.broadcast_to(unit, (1, 128))

    got2[g], scale2[g] = owned(g)

    for p in ORDER[1:]:
        where = lax.bitwise_xor(g, p)
        out2[where], scale_out[where] = owned(where)
        for copy in home(p):
            copy.start()

    for p in ORDER[1:]:
        for copy in home(p):
            copy.wait()
        piece(1, p).wait_send()
    for p in ORDER[GRP - LAG :]:
        piece(0, p).wait_send()
    for copy in sends:
        copy.wait_send()
    near(0, GRP + s, {"slab": 1 - s}).wait_send()

    @pl.when(c < NCOL - 1)
    def _():
        near(1, GRP + 2, {"col": c + 1}).wait_send()

    @pl.when(c > 0)
    def _():
        near(2, GRP + 3, {"col": c - 1}).wait_send()


def unpack(got, scale, out):
    for m in range(GRP):
        v = decode(got[m]) * scale[m][0:1, 0:1]
        flat = v.T
        for h in range(2):
            out[GRP * h + m] = flat[B * h : B * (h + 1), :]


def per_device(fine_blocks, prolong, column_ids, aggregate_ids, live_rows):
    vmem = pl.BlockSpec(memory_space=pltpu.VMEM)
    hbm = pl.BlockSpec(memory_space=pltpu.HBM)
    dma = pltpu.SemaphoreType.DMA
    coded, scale = pl.pallas_call(
        kernel,
        out_shape=[
            jax.ShapeDtypeStruct((GRP, WIDTH, 256), jnp.int16),
            jax.ShapeDtypeStruct((GRP, 1, 128), F32),
        ],
        in_specs=[hbm] * 5,
        out_specs=[vmem, vmem],
        scratch_shapes=[
            pltpu.VMEM((RB, B, B), BF16),
            pltpu.VMEM((RB, KA), jnp.int32),
            pltpu.SMEM((RB, KA), jnp.int32),
            pltpu.SMEM((RB,), jnp.int32),
            pltpu.SMEM((1,), jnp.int32),
            pltpu.VMEM((GRP * WIDTH, BATCH * 128), BF16),
            pltpu.VMEM((BATCH * 128, 256), BF16),
            pltpu.VMEM((BATCH * 128, 256), BF16),
            pltpu.VMEM((RB, KA, B, B), BF16),
            pltpu.VMEM((GRP + 4, MSG, 128), BF16),
            pltpu.VMEM((2 * TILES, B, 128), BF16),
            pltpu.VMEM((RB, B, B), BF16),
            pltpu.VMEM((RB, KP // 2, 2 * B, 128), BF16),
            pltpu.VMEM((8, 128), jnp.int32),
            pltpu.VMEM((2 * GRP * CR, 128), F32),
            pltpu.VMEM((CHUNKS, GRP, CR, 256), jnp.int16),
            pltpu.VMEM((CHUNKS, GRP, CR, 256), jnp.int16),
            pltpu.VMEM((CHUNKS, 8, 128), F32),
            pltpu.VMEM((GRP * WIDTH, 256), F32),
            pltpu.VMEM((GRP, WIDTH, 256), jnp.int16),
            pltpu.VMEM((GRP, 1, 128), F32),
            dma((5,)),
            dma((RB,)),
            dma((32,)),
            dma((32,)),
            dma((3,)),
            dma((3,)),
            dma((CHUNKS, GRP)),
            dma((CHUNKS, GRP)),
            dma((GRP,)),
            dma((GRP,)),
            dma((GRP,)),
            dma((GRP,)),
        ],
        compiler_params=pltpu.CompilerParams(
            collective_id=0, has_side_effects=True, vmem_limit_bytes=58 * 2**20
        ),
    )(fine_blocks, prolong, column_ids, aggregate_ids, live_rows)
    out = pl.pallas_call(
        unpack,
        grid=(2,),
        out_shape=jax.ShapeDtypeStruct((B, B, WIDTH), F32),
        in_specs=[
            pl.BlockSpec((GRP, WIDTH, 128), lambda j: (0, 0, j)),
            pl.BlockSpec((GRP, 1, 128), lambda j: (0, 0, 0)),
        ],
        out_specs=pl.BlockSpec((2 * GRP, B, WIDTH), lambda j: (j, 0, 0)),
        compiler_params=pltpu.CompilerParams(vmem_limit_bytes=58 * 2**20),
    )(coded, scale)
    return out.transpose(2, 0, 1)[None]


def solution(mesh):
    rows = ("slab", "grp", "col")
    return jax.shard_map(
        per_device,
        mesh=mesh,
        in_specs=(
            P(rows, None, None, None),
            P(rows, None, None),
            P(rows, None),
            P(rows),
            P(rows),
        ),
        out_specs=P(rows, None, None, None),
        check_vma=False,
    )
```

```python
import functools

import jax
import jax.numpy as jnp
from jax import lax
from jax.experimental import pallas as pl
from jax.experimental.pallas import tpu as pltpu
from jax.sharding import PartitionSpec as P

MESH = pl.DeviceIdType.MESH
GRP, SIDE, NCOL = 16, 4, 8
RB, KA, B = 8, 27, 64
KP = 28
CHUNKS, PER = 2, 4
CR = KP * PER
WIDTH = 80
TILES = 160
EARLY = 5
ORDER = (0, 10, 6, 9, 11, 14, 2, 5, 7, 8, 13, 15, 1, 3, 4, 12)
LAG = 3
BATCH = 4
MSG = 272
HALF = (pl.ds(0, 144), pl.ds(144, 128))
FULL = 32760.0
F32, BF16 = jnp.float32, jnp.bfloat16


def root(x, inverse):
    t = x * inverse
    return t * lax.rsqrt(jnp.maximum(jnp.abs(t), 1e-30))


def short(y):
    return y.astype(jnp.int32).astype(jnp.int16)


def decode(v):
    v = v.astype(F32)
    return v * (jnp.abs(v) + 1.0)


def remote(src, dst, send, recv, where):
    return pltpu.make_async_remote_copy(
        src_ref=src, dst_ref=dst, send_sem=send, recv_sem=recv, device_id=where, device_id_type=MESH
    )


def kernel(
    blocks_hbm, prolong_hbm, ids_hbm, aggs_hbm, live_hbm,
    got2, scale2,
    prolong, ids_vec, ids, aggs, live, pick, high, lower, blocks, tiles, table, flipped, u, ids_row, stage, out1, got1, keys, total, out2, scale_out,
    small_sem, block_sem, ag_send, ag_recv, near_send, near_recv,
    d_send, d_recv, e_send, e_recv, f_send, f_recv,
):
    s, g, c = lax.axis_index("slab"), lax.axis_index("grp"), lax.axis_index("col")
    gy, gx = g // SIDE, lax.rem(g, SIDE)
    bar = pltpu.get_barrier_semaphore()
    for p in range(1, GRP):
        pl.semaphore_signal(bar, inc=1, device_id={"grp": lax.rem(g + p, GRP)}, device_id_type=MESH)
    pl.semaphore_signal(bar, inc=1, device_id={"slab": 1 - s}, device_id_type=MESH)

    @pl.when(c > 0)
    def _():
        pl.semaphore_signal(bar, inc=1, device_id={"col": c - 1}, device_id_type=MESH)

    @pl.when(c < NCOL - 1)
    def _():
        pl.semaphore_signal(bar, inc=1, device_id={"col": c + 1}, device_id_type=MESH)

    small = [
        pltpu.make_async_copy(src, dst, small_sem.at[n])
        for n, (src, dst) in enumerate(
            ((prolong_hbm, prolong), (live_hbm, live), (aggs_hbm, aggs), (ids_hbm, ids_vec), (ids_hbm, ids))
        )
    ]
    for copy in small:
        copy.start()

    def block_copy(i):
        return pltpu.make_async_copy(blocks_hbm.at[i], blocks.at[i], block_sem.at[i])

    for i in range(RB):
        block_copy(i).start()
    for copy in small[:3]:
        copy.wait()

    alive = jnp.full((B, B), live[0], jnp.int32)
    for r in range(0, RB, 2):
        left, right = (
            jnp.where(alive > r + d, prolong[r + d].astype(F32), 0.0) for d in range(2)
        )
        tiles[g, 32 * r : 32 * r + B, :] = jnp.concatenate([left, right], axis=1).astype(BF16)
        flipped[r] = left.T.astype(BF16)
        flipped[r + 1] = right.T.astype(BF16)
    sub16 = lax.broadcasted_iota(jnp.int32, (16, 128), 0)
    agg_rows = jnp.zeros((16, 128), F32)
    for r in range(RB):
        agg_rows = jnp.where(sub16 == r, aggs[r].astype(F32), agg_rows)
    tiles[g, 256:MSG, :] = agg_rows.astype(BF16)

    tiles[GRP + s] = jnp.zeros((MSG, 128), BF16)

    @pl.when(c == 0)
    def _():
        tiles[GRP + 2] = jnp.zeros((MSG, 128), BF16)

    @pl.when(c == NCOL - 1)
    def _():
        tiles[GRP + 3] = jnp.zeros((MSG, 128), BF16)

    def u_row(i, carry):
        block_copy(i).wait()
        for k in range(0, KP, 2):
            left = jnp.dot(flipped[i], blocks[i, k], preferred_element_type=F32)
            if k + 1 < KA:
                right = jnp.dot(flipped[i], blocks[i, k + 1], preferred_element_type=F32)
            else:
                right = jnp.zeros((B, B), F32)
            value = jnp.concatenate([left, right], axis=1)
            high = value.astype(BF16)
            u[i, k // 2, 0:B, :] = high
            u[i, k // 2, B : 2 * B, :] = (value - high.astype(F32)).astype(BF16)
        return carry

    lax.fori_loop(0, EARLY, u_row, 0)
    cols = (c + NCOL - 1) // NCOL + (2 * NCOL - 2 - c) // NCOL
    pl.semaphore_wait(bar, GRP + cols)

    sends = []

    def spread(slot, half, y, x, source):
        copy = remote(
            tiles.at[slot, HALF[half]],
            tiles.at[slot, HALF[half]],
            ag_send.at[len(sends)],
            ag_recv.at[source * 2 + half],
            {"grp": y * SIDE + x},
        )
        copy.start()
        sends.append(copy)

    def arrived(dy, dx, half):
        slot = lax.rem(gy + dy, SIDE) * SIDE + lax.rem(gx + dx, SIDE)
        remote(
            tiles.at[slot, HALF[half]], tiles.at[slot, HALF[half]],
            ag_send.at[0], ag_recv.at[(dy * SIDE + dx) * 2 + half], {"grp": lax.rem(g + 1, GRP)},
        ).wait_recv()
        return slot

    for d in (1, 3, 2):
        back = SIDE - d
        spread(g, 0, gy, lax.rem(gx + d, SIDE), back)
        spread(g, 1, lax.rem(gy + d, SIDE), gx, back * SIDE)
    for d in (1, 3, 2):
        back = SIDE - d
        spread(g, 1, gy, lax.rem(gx + d, SIDE), back)
        spread(g, 0, lax.rem(gy + d, SIDE), gx, back * SIDE)

    def near(k, slot, where):
        return remote(tiles.at[g], tiles.at[slot], near_send.at[k], near_recv.at[k], where)

    near(0, GRP + s, {"slab": 1 - s}).start()

    @pl.when(c < NCOL - 1)
    def _():
        near(1, GRP + 2, {"col": c + 1}).start()

    @pl.when(c > 0)
    def _():
        near(2, GRP + 3, {"col": c - 1}).start()

    wide = lax.broadcasted_iota(jnp.int32, (B, 128), 1) < B
    first_half = jnp.where(wide, 1.0, 0.0).astype(BF16)
    second_half = jnp.where(wide, 0.0, 1.0).astype(BF16)

    def unfold(slot):
        def pair(n, carry):
            both = tiles[slot, pl.ds(pl.multiple_of(n * B, B), B), :]
            turned = pltpu.roll(both.astype(F32), B, 1).astype(BF16)
            at = slot * RB + 2 * n
            table[at] = both * first_half
            table[at + 1] = turned * first_half
            table[TILES + at] = turned * second_half
            table[TILES + at + 1] = both * second_half
            return carry

        lax.fori_loop(0, RB // 2, pair, 0)

    for n, e in enumerate((1, 3, 2)):
        lax.fori_loop(EARLY + n, EARLY + n + 1, u_row, 0)
        slot = arrived(0, e, 0)
        for d in (1, 3, 2):
            spread(slot, 0, lax.rem(gy + d, SIDE), gx, (SIDE - d) * SIDE + e)
        slot = arrived(e, 0, 1)
        for d in (1, 3, 2):
            spread(slot, 1, gy, lax.rem(gx + d, SIDE), e * SIDE + SIDE - d)

    lax.fori_loop(EARLY + 3, RB, u_row, 0)
    unfold(g)
    for e in (1, 3, 2):
        unfold(arrived(0, e, 1))
        unfold(arrived(e, 0, 0))
    near(0, GRP + 1 - s, {"slab": 1 - s}).wait_recv()

    @pl.when(c > 0)
    def _():
        near(1, GRP + 2, {"col": c - 1}).wait_recv()

    @pl.when(c < NCOL - 1)
    def _():
        near(2, GRP + 3, {"col": c + 1}).wait_recv()

    for slot in range(GRP, GRP + 4):
        unfold(slot)
    for e in (1, 3, 2):
        for f in (1, 3, 2):
            arrived(e, f, 0)
            unfold(arrived(e, f, 1))

    for copy in small[3:]:
        copy.wait()
    ids_row[...] = jnp.full((8, 128), -1, jnp.int32)
    ids_row[:, 0:KA] = ids_vec[...]
    lane = lax.broadcasted_iota(jnp.int32, (8, 128), 1)
    sub = lax.broadcasted_iota(jnp.int32, (8, 128), 0)
    for ch in range(CHUNKS):
        q = jnp.full((8, 128), -1, jnp.int32)
        owner = jnp.zeros((8, 128), F32)
        for ii in range(PER):
            i = PER * ch + ii
            row = jnp.broadcast_to(ids_row[i : i + 1, :], (8, 128))
            inside = (lane >= KP * ii) & (lane < KP * (ii + 1))
            q = jnp.where(inside, pltpu.roll(row, KP * ii, 1) if ii else row, q)
            owner = jnp.where(inside, aggs[i].astype(F32), owner)
        slot = jnp.zeros((8, 128), F32)
        for d in range(GRP + 4):
            base = 0 if d < GRP else (d - GRP + 1) * GRP
            named = tiles[d, 256:MSG, :].astype(F32)[0:8]
            slot = slot + jnp.where(q == sub + 8 * d, named + base, 0.0)
        slot = jnp.broadcast_to(jnp.sum(slot, axis=0, keepdims=True), (8, 128))
        key = jnp.where(q < 0, -1.0, owner * WIDTH + slot)
        keys[ch] = key

    low = lax.broadcasted_iota(jnp.int32, (8, 128), 1) < B

    def piece(ch, p):
        where = lax.bitwise_xor(g, p)
        return remote(out1.at[ch, where], got1.at[ch, g], d_send.at[ch, p], d_recv.at[ch, p], {"grp": where})

    high[...] = jnp.zeros_like(high)
    lower[...] = jnp.zeros_like(lower)
    pick[...] = jnp.zeros_like(pick)

    def load(ch, n, source):
        v = decode(got1[ch, source])
        top = v.astype(BF16)
        high[n * 128 : n * 128 + CR, :] = top
        lower[n * 128 : n * 128 + CR, :] = (v - top.astype(F32)).astype(BF16)
        key = got1[ch, source, 16:32, 0:128].astype(F32)[KP - 17 : KP - 16, 0:CR]
        unit = jnp.exp2(got1[ch, source, 48:64, 0:128].astype(F32)[2 * KP - 49 : 2 * KP - 48, 0:CR])
        for r in range(0, GRP * WIDTH, 64):
            row = lax.broadcasted_iota(jnp.int32, (64, CR), 0).astype(F32) + float(r)
            pick[r : r + 64, n * 128 : n * 128 + CR] = jnp.where(row == key, unit, 0.0).astype(BF16)

    def batch(ch, first, count):
        for n in range(count):
            p = ORDER[first + n]
            if p:
                piece(ch, p).wait_recv()
            load(ch, n, lax.bitwise_xor(g, p))
        depth = 128 * count
        value = jnp.dot(pick[:, 0:depth], high[0:depth, :], preferred_element_type=F32)
        value = value + jnp.dot(pick[:, 0:depth], lower[0:depth, :], preferred_element_type=F32)
        if ch or first:
            total[...] += value
        else:
            total[...] = value

    row_of = lax.broadcasted_iota(jnp.int32, (CR, 128), 0)
    for ch in range(CHUNKS):
        def t_row(ii, scales, ch=ch):
            i = PER * ch + ii
            top = jnp.zeros((8, 128), F32)
            for k in range(0, KP, 2):
                weights = jnp.concatenate(
                    [table[ids[i, k]], table[TILES + ids[i, min(k + 1, KA - 1)]]], axis=0
                )
                both = jnp.dot(u[i, k // 2], weights, preferred_element_type=F32)
                value = both[0:B] + both[B : 2 * B]
                top = jnp.maximum(top, jnp.max(jnp.abs(value).reshape(8, 8, 128), axis=0))
                for half in range(2):
                    for w in range(2):
                        first = value[32 * w + 8 * half : 32 * w + 8 * half + 8]
                        second = value[32 * w + 16 + 8 * half : 32 * w + 24 + 8 * half]
                        at = CR * (GRP * w + 8 * half) + KP * ii + k
                        stage[pl.ds(at, 8, stride=CR), :] = jnp.where(low, first, pltpu.roll(second, B, 1))
                        stage[pl.ds(at + 1, 8, stride=CR), :] = jnp.where(low, pltpu.roll(first, B, 1), second)
            most = jnp.max(jnp.max(top, axis=1, keepdims=True), axis=0, keepdims=True)
            most = jnp.broadcast_to(most, (8, 128))
            power = jnp.ceil(jnp.log2(jnp.maximum(most, 1e-25) * (1.004 / (FULL * FULL))))
            return tuple(jnp.where(ii == n, power, scales[n]) for n in range(PER))

        scales = lax.fori_loop(0, PER, t_row, tuple(jnp.zeros((8, 128), F32) for _ in range(PER)))
        powers = jnp.zeros((8, 128), F32)
        inverse = jnp.zeros((CR, 128), F32)
        for ii in range(PER):
            powers = jnp.where((lane >= KP * ii) & (lane < KP * (ii + 1)), scales[ii], powers)
            inverse = jnp.where(row_of >= KP * ii, jnp.exp2(-scales[ii])[0:1], inverse)

        def coded(where, ch=ch, inverse=inverse, powers=powers):
            first = root(stage[pl.ds(pl.multiple_of(where * CR, 16), CR), :], inverse)
            second = root(stage[pl.ds(pl.multiple_of((GRP + where) * CR, 16), CR), :], inverse)
            first = jnp.where(row_of == KP - 1, keys[ch][0:1], first)
            first = jnp.where(row_of == 2 * KP - 1, powers[0:1], first)
            return jnp.concatenate([short(first), short(second)], axis=1)

        got1[ch, g] = coded(g)
        for n in range(1, GRP):
            p = ORDER[n]
            where = lax.bitwise_xor(g, p)
            out1[ch, where] = coded(where)
            if ch and n > LAG:
                piece(0, ORDER[n - LAG]).wait_send()
            piece(ch, p).start()
            if ch and n % BATCH == BATCH - 1:
                batch(0, n - BATCH + 1, BATCH)

    batch(1, 0, 4)
    batch(1, 4, 4)
    batch(1, 8, 4)
    batch(1, 12, 2)
    batch(1, 14, 2)

    def home(p):
        where = lax.bitwise_xor(g, p)
        return (
            remote(out2.at[where], got2.at[g], e_send.at[p], e_recv.at[p], {"grp": where}),
            remote(scale_out.at[where], scale2.at[g], f_send.at[p], f_recv.at[p], {"grp": where}),
        )

    def owned(where):
        value = total[pl.ds(pl.multiple_of(where * WIDTH, 16), WIDTH), :]
        most = jnp.max(jnp.max(jnp.abs(value), axis=1, keepdims=True), axis=0, keepdims=True)
        unit = jnp.maximum(most, 1e-25) * (1.004 / (FULL * FULL))
        return short(root(value, 1.0 / unit)), jnp.broadcast_to(unit, (1, 128))

    got2[g], scale2[g] = owned(g)

    for p in ORDER[1:]:
        where = lax.bitwise_xor(g, p)
        out2[where], scale_out[where] = owned(where)
        for copy in home(p):
            copy.start()

    for p in ORDER[1:]:
        for copy in home(p):
            copy.wait()
        piece(1, p).wait_send()
    for p in ORDER[GRP - LAG :]:
        piece(0, p).wait_send()
    for copy in sends:
        copy.wait_send()
    near(0, GRP + s, {"slab": 1 - s}).wait_send()

    @pl.when(c < NCOL - 1)
    def _():
        near(1, GRP + 2, {"col": c + 1}).wait_send()

    @pl.when(c > 0)
    def _():
        near(2, GRP + 3, {"col": c - 1}).wait_send()


def unpack(got, scale, out):
    for m in range(GRP):
        v = decode(got[m]) * scale[m][0:1, 0:1]
        flat = v.T
        for h in range(2):
            out[GRP * h + m] = flat[B * h : B * (h + 1), :]


def per_device(fine_blocks, prolong, column_ids, aggregate_ids, live_rows):
    vmem = pl.BlockSpec(memory_space=pltpu.VMEM)
    hbm = pl.BlockSpec(memory_space=pltpu.HBM)
    dma = pltpu.SemaphoreType.DMA
    coded, scale = pl.pallas_call(
        kernel,
        out_shape=[
            jax.ShapeDtypeStruct((GRP, WIDTH, 256), jnp.int16),
            jax.ShapeDtypeStruct((GRP, 1, 128), F32),
        ],
        in_specs=[hbm] * 5,
        out_specs=[vmem, vmem],
        scratch_shapes=[
            pltpu.VMEM((RB, B, B), BF16),
            pltpu.VMEM((RB, KA), jnp.int32),
            pltpu.SMEM((RB, KA), jnp.int32),
            pltpu.SMEM((RB,), jnp.int32),
            pltpu.SMEM((1,), jnp.int32),
            pltpu.VMEM((GRP * WIDTH, BATCH * 128), BF16),
            pltpu.VMEM((BATCH * 128, 256), BF16),
            pltpu.VMEM((BATCH * 128, 256), BF16),
            pltpu.VMEM((RB, KA, B, B), BF16),
            pltpu.VMEM((GRP + 4, MSG, 128), BF16),
            pltpu.VMEM((2 * TILES, B, 128), BF16),
            pltpu.VMEM((RB, B, B), BF16),
            pltpu.VMEM((RB, KP // 2, 2 * B, 128), BF16),
            pltpu.VMEM((8, 128), jnp.int32),
            pltpu.VMEM((2 * GRP * CR, 128), F32),
            pltpu.VMEM((CHUNKS, GRP, CR, 256), jnp.int16),
            pltpu.VMEM((CHUNKS, GRP, CR, 256), jnp.int16),
            pltpu.VMEM((CHUNKS, 8, 128), F32),
            pltpu.VMEM((GRP * WIDTH, 256), F32),
            pltpu.VMEM((GRP, WIDTH, 256), jnp.int16),
            pltpu.VMEM((GRP, 1, 128), F32),
            dma((5,)),
            dma((RB,)),
            dma((32,)),
            dma((32,)),
            dma((3,)),
            dma((3,)),
            dma((CHUNKS, GRP)),
            dma((CHUNKS, GRP)),
            dma((GRP,)),
            dma((GRP,)),
            dma((GRP,)),
            dma((GRP,)),
        ],
        compiler_params=pltpu.CompilerParams(
            collective_id=0, has_side_effects=True, vmem_limit_bytes=58 * 2**20
        ),
    )(fine_blocks, prolong, column_ids, aggregate_ids, live_rows)
    out = pl.pallas_call(
        unpack,
        grid=(2,),
        out_shape=jax.ShapeDtypeStruct((B, B, WIDTH), F32),
        in_specs=[
            pl.BlockSpec((GRP, WIDTH, 128), lambda j: (0, 0, j)),
            pl.BlockSpec((GRP, 1, 128), lambda j: (0, 0, 0)),
        ],
        out_specs=pl.BlockSpec((2 * GRP, B, WIDTH), lambda j: (j, 0, 0)),
        compiler_params=pltpu.CompilerParams(vmem_limit_bytes=58 * 2**20),
    )(coded, scale)
    return out.transpose(2, 0, 1)[None]


def solution(mesh):
    rows = ("slab", "grp", "col")
    return jax.shard_map(
        per_device,
        mesh=mesh,
        in_specs=(
            P(rows, None, None, None),
            P(rows, None, None),
            P(rows, None),
            P(rows),
            P(rows),
        ),
        out_specs=P(rows, None, None, None),
        check_vma=False,
    )
```
